1024 devices in a mesh: section: 4 (over z_hi), expert: 64 (over x, y, core), dp: 4 (over z_lo).
Axes of the slice: x: 4, y: 8, z: 16 (z_hi: 4, z_lo: 4; z = z_hi * 4 + z_lo), core: 2. Of those that a mesh axis runs over, the one named last changes fastest.
Arguments:
- fwd_act: bfloat16 [4, 1024, 7168], P('section', 'expert', 'dp'), may hold values from -6 to 6
- fwd_routes: int32 [4, 1024, 8], P('section', 'expert'), may hold values from 0 to 63, all different within a row; in each aligned block of 16 rows (0 to 15, 16 to 31, ..., all dimensions but the last counted through in order) at most 4 rows name the same one
- fwd_probs: float32 [4, 1024, 8], P('section', 'expert'), may hold values from 0.02 to 0.5
- bwd_grad: bfloat16 [4, 1024, 7168], P('section', 'expert', 'dp'), may hold values from -6 to 6
- bwd_routes: int32 [4, 1024, 8], P('section', 'expert'), may hold values from 0 to 63, all different within a row; in each aligned block of 16 rows (0 to 15, 16 to 31, ..., all dimensions but the last counted through in order) at most 4 rows name the same one
- bwd_probs: float32 [4, 1024, 8], P('section', 'expert'), may hold values from 0.02 to 0.5
- w_up: bfloat16 [64, 7168, 1024], P('expert', 'dp'), may hold values from -0.0625 to 0.0625
- w_down: bfloat16 [64, 1024, 7168], P('expert', None, 'dp'), may hold values from -0.1875 to 0.1875
- act_stash: bfloat16 [4, 64, 256, 1024], P('section', 'expert'), may hold values from -6 to 6
Outputs:
- fwd_out: bfloat16 [4, 1024, 7168], P('section', 'expert', 'dp')
- bwd_out: bfloat16 [4, 1024, 7168], P('section', 'expert', 'dp')
The draws below stay inside these ranges and needn't reach their ends.
Inputs may be any that keep to these rules, and one draw needn't show every extreme that they name: `fwd_routes`: each row names 8 different experts. Among the 16 rows of one expert group of one section no expert is named more than 4 times, a bound that some block reaches. `bwd_routes`: each row names 8 different experts. Among the 16 rows of one expert group of one section no expert is named more than 4 times, a bound that some block reaches.
All inputs are finite; a program needn't handle non-finite values.
Results may differ from the reference program's by a relative error of at most 0.0064.
Values may be sent and summed in bfloat16 or wider, within the bound.
No kernel may reach another device: no remote copies, remote signals or barrier semaphores. Data moves between devices by JAX's collectives and lax.ppermute only.
A program may use at most 32 MiB of HBM per device.

```python
import math
import jax
import jax.numpy as jnp
import numpy as np
from jax import lax

D = 7168
FF = 1024
TOK = 16
EXPERTS = 64
TOPK = 8
CAP = 4
TOKENS = 1024
N_SECTION = 4


def levels(own_key, extent, cuts, smallest, largest):
    level, own = 1.0, jax.random.fold_in(own_key, 6)
    for dim, parts in cuts:
        draws = jnp.exp(jax.random.uniform(jax.random.fold_in(own, dim), (parts,), jnp.float32, smallest / len(cuts), largest / len(cuts)))
        level = level * jnp.repeat(draws, extent[dim] // parts).reshape([-1 if axis == dim else 1 for axis in range(len(extent))])
    return level


def deal_out(key, own, number, rows, amount, top, reach, skew):
    ranking = jax.random.permutation(key, amount)
    crowded, usual = load_shares(amount, rows * top, reach, skew, True), load_shares(amount, rows * top, reach, skew, False)
    places = jnp.arange(amount)

    def named(lengths, offset_by):
        used = int((lengths > 0).sum())
        fixed = max(1, used // 4)
        moved = fixed + (places - fixed + offset_by * (used - fixed)) % max(1, amount - fixed)
        return jnp.zeros((amount,), jnp.int32).at[ranking[jnp.where(places < fixed, places, moved)]].set(jnp.asarray(lengths, jnp.int32))

    lengths = jnp.where(number % 4 == 0, named(crowded, number // 4), named(usual, number - number // 4 - 1))
    mixed = jax.random.permutation(jax.random.fold_in(own, 3), amount)
    giver, taker = mixed[0:amount // 2 * 2:2], mixed[1:amount // 2 * 2:2]
    margin = jnp.minimum(lengths[giver] - 1, reach - lengths[taker]) // 2
    margin = jnp.where((giver == ranking[0]) | (taker == ranking[0]) | (lengths[taker] == 0), 0, jnp.maximum(margin, 0))
    moved = jax.random.randint(jax.random.fold_in(own, 4), (amount // 2,), 0, 1 << 20) % (margin + 1)
    lengths = lengths.at[giver].add(-moved).at[taker].add(moved)
    labels = jnp.searchsorted(jnp.cumsum(lengths), jnp.arange(rows * top), side="right").astype(jnp.int32)
    table = labels.reshape(top, rows).T
    table = table[jax.random.permutation(jax.random.fold_in(own, 1), rows)]
    offset_by = jax.random.randint(jax.random.fold_in(own, 2), (rows, 1), 0, top)
    return jnp.take_along_axis(table, (jnp.arange(top)[None, :] + offset_by) % top, axis=1)


def load_shares(number_of, total, reach, slope, full):
    loads = [(1 << 20) // math.isqrt(standing ** slope) + 1 for standing in range(1, number_of + 1)]
    largest = reach if full else min(reach, max(-(-total // number_of), total * loads[0] // sum(loads)))
    least = 1 if total - largest >= number_of - 1 else 0
    holding, surplus = [largest] + [least] * (number_of - 1), total - largest - least * (number_of - 1)
    while surplus > 0:
        free = [i for i in range(1, number_of) if holding[i] < largest] or [i for i in range(1, number_of) if holding[i] < reach]
        pool, left = sum([loads[i] for i in free]), surplus
        for i in free:
            more = min(reach - holding[i], max(1, left * loads[i] // pool), surplus)
            holding[i] = holding[i] + more
            surplus = surplus - more
    return np.array(holding)


def bell_draw(rng, shape, width, bound, cuts=(), kind=jnp.bfloat16):
    level = levels(rng, shape, cuts, -0.22, 0.18) if cuts else 1.0
    entries = jax.random.normal(rng, shape, jnp.float32) * width * level
    return jnp.minimum(jnp.maximum(entries, -bound), bound).astype(kind)


def setup_inputs(seed: int = 0) -> dict:
    streams_of = jax.random.split(jax.random.key(seed), 10)
    fwd_act = bell_draw(streams_of[0], (N_SECTION, TOKENS, D), 1.0, 6.0, ((0, 4), (1, 64), (2, 4)))
    fwd_routes_keys = jax.random.split(jax.random.fold_in(streams_of[1], 1), N_SECTION * TOKENS // TOK)
    fwd_routes_turns = jax.random.permutation(jax.random.fold_in(streams_of[1], 3), N_SECTION * TOKENS // TOK)
    fwd_routes = jax.vmap(lambda own, number: deal_out(jax.random.fold_in(streams_of[1], 2), own, number, TOK, EXPERTS, TOPK, CAP, 2))(fwd_routes_keys, fwd_routes_turns).reshape((N_SECTION, TOKENS, TOPK))
    fwd_probs = jnp.clip(jnp.exp(math.log(0.5) - 3.218876 * jax.random.uniform(streams_of[2], (N_SECTION, TOKENS, TOPK), jnp.float32) ** levels(streams_of[2], (N_SECTION, TOKENS, TOPK), ((0, 4), (1, 64)), -0.2, 0.2)), 0.02, 0.5)
    bwd_grad = bell_draw(streams_of[3], (N_SECTION, TOKENS, D), 1.0, 6.0, ((0, 4), (1, 64), (2, 4)))
    bwd_routes_keys = jax.random.split(jax.random.fold_in(streams_of[4], 1), N_SECTION * TOKENS // TOK)
    bwd_routes_turns = jax.random.permutation(jax.random.fold_in(streams_of[4], 3), N_SECTION * TOKENS // TOK)
    bwd_routes = jax.vmap(lambda own, number: deal_out(jax.random.fold_in(streams_of[4], 2), own, number, TOK, EXPERTS, TOPK, CAP, 2))(bwd_routes_keys, bwd_routes_turns).reshape((N_SECTION, TOKENS, TOPK))
    bwd_probs = jnp.clip(jnp.exp(math.log(0.5) - 3.218876 * jax.random.uniform(streams_of[5], (N_SECTION, TOKENS, TOPK), jnp.float32) ** levels(streams_of[5], (N_SECTION, TOKENS, TOPK), ((0, 4), (1, 64)), -0.2, 0.2)), 0.02, 0.5)
    w_up = bell_draw(streams_of[6], (EXPERTS, D, FF), D ** -0.5, 0.0625, ((0, 64), (1, 4)))
    w_down = bell_draw(streams_of[7], (EXPERTS, FF, D), FF ** -0.5, 0.1875, ((0, 64), (2, 4)))
    act_stash = bell_draw(streams_of[8], (N_SECTION, EXPERTS, EXPERTS * CAP, FF), 1.5, 6.0, ((0, 4), (1, 64)))
    return {"fwd_act": fwd_act, "fwd_routes": fwd_routes, "fwd_probs": fwd_probs, "bwd_grad": bwd_grad, "bwd_routes": bwd_routes, "bwd_probs": bwd_probs, "w_up": w_up, "w_down": w_down, "act_stash": act_stash}


def slot_targets(route_rows, experts, capacity):
    flat_routes = route_rows.reshape(-1).astype(jnp.int32)
    matches = (flat_routes[:, None] == jnp.arange(experts, dtype=jnp.int32)[None, :]).astype(jnp.int32)
    before = jnp.cumsum(matches, axis=0) - matches
    slot_rank = jnp.sum(before * matches, axis=1)
    return (flat_routes * capacity + slot_rank).astype(jnp.int32)


def silu_slope(pre_act):
    squash = jax.nn.sigmoid(pre_act)
    return squash * (1.0 + pre_act * (1.0 - squash))


def place_rows(token_rows, targets, slot_count):
    matches = targets[None, :] == jnp.arange(slot_count, dtype=jnp.int32)[:, None]
    positions = jnp.arange(targets.shape[0], dtype=jnp.int32)[None, :]
    source = jnp.sum(jnp.where(matches, positions, 0), axis=1).astype(jnp.int32)
    filled = jnp.any(matches, axis=1)
    return jnp.where(filled[:, None], token_rows[source], jnp.zeros((), token_rows.dtype))


def pick_rows(result_rows, targets):
    return result_rows[targets]


def reference(fwd_act, fwd_routes, fwd_probs, bwd_grad, bwd_routes, bwd_probs, w_up, w_down, act_stash):
    sections = N_SECTION
    experts = EXPERTS
    capacity = CAP
    top_count = TOPK
    slot_count = experts * capacity
    arriving = jnp.roll(fwd_act, 1, axis=0).reshape(sections, experts, TOK, D)
    incoming = jnp.roll(bwd_grad, -1, axis=0).reshape(sections, experts, TOK, D)

    def targets_of(route_rows):
        return slot_targets(route_rows, experts, capacity)

    targets_fwd = jax.vmap(jax.vmap(targets_of))(fwd_routes.reshape(sections, experts, TOK, top_count))
    targets_bwd = jax.vmap(jax.vmap(targets_of))(bwd_routes.reshape(sections, experts, TOK, top_count))
    rows_fwd = jnp.repeat(arriving, top_count, axis=2)
    probs_b = bwd_probs.reshape(sections, experts, TOK, top_count, 1)
    weighted = (probs_b * incoming[:, :, :, None, :].astype(jnp.float32)).astype(jnp.bfloat16)
    weighted = weighted.reshape(sections, experts, TOK * top_count, D)

    def placed(token_rows, targets):
        return place_rows(token_rows, targets, slot_count)

    sent_fwd = jax.vmap(jax.vmap(placed))(rows_fwd, targets_fwd)
    sent_bwd = jax.vmap(jax.vmap(placed))(weighted, targets_bwd)
    recv_fwd = sent_fwd.reshape(sections, experts, experts, capacity, D).transpose(2, 0, 1, 3, 4)
    recv_fwd = recv_fwd.reshape(experts, sections, slot_count, D)
    recv_bwd = sent_bwd.reshape(sections, experts, experts, capacity, D).transpose(2, 0, 1, 3, 4)
    recv_bwd = recv_bwd.reshape(experts, sections, slot_count, D)
    stash_by_expert = act_stash.transpose(1, 0, 2, 3)

    def expert_pass(members):
        up_weight, down_weight, fwd_rows, bwd_rows, stash_rows = members
        pre_fwd = jnp.dot(fwd_rows.reshape(-1, D), up_weight, preferred_element_type=jnp.float32)
        hidden_fwd = jax.nn.silu(pre_fwd).astype(jnp.bfloat16)
        out_rows = jnp.dot(hidden_fwd, down_weight, preferred_element_type=jnp.float32).astype(jnp.bfloat16)
        grad_hidden = lax.dot_general(bwd_rows.reshape(-1, D), down_weight, (((1,), (1,)), ((), ())), preferred_element_type=jnp.float32)
        grad_pre = (grad_hidden * silu_slope(stash_rows.reshape(-1, FF).astype(jnp.float32))).astype(jnp.bfloat16)
        grad_rows = lax.dot_general(grad_pre, up_weight, (((1,), (1,)), ((), ())), preferred_element_type=jnp.float32).astype(jnp.bfloat16)
        return out_rows.reshape(fwd_rows.shape), grad_rows.reshape(bwd_rows.shape)

    out_by_expert, grad_by_expert = lax.map(expert_pass, (w_up, w_down, recv_fwd, recv_bwd, stash_by_expert))
    back_fwd = out_by_expert.reshape(experts, sections, experts, capacity, D).transpose(1, 2, 0, 3, 4)
    back_fwd = back_fwd.reshape(sections, experts, slot_count, D)
    back_bwd = grad_by_expert.reshape(experts, sections, experts, capacity, D).transpose(1, 2, 0, 3, 4)
    back_bwd = back_bwd.reshape(sections, experts, slot_count, D)
    taken_fwd = jax.vmap(jax.vmap(pick_rows))(back_fwd, targets_fwd)
    taken_bwd = jax.vmap(jax.vmap(pick_rows))(back_bwd, targets_bwd)
    probs_f = fwd_probs.reshape(sections, experts, TOK, top_count, 1)
    fwd_out = jnp.sum(probs_f * taken_fwd.reshape(sections, experts, TOK, top_count, D).astype(jnp.float32), axis=3)
    bwd_out = jnp.sum(taken_bwd.reshape(sections, experts, TOK, top_count, D).astype(jnp.float32), axis=3)
    fwd_out = fwd_out.reshape(sections, experts * TOK, D).astype(jnp.bfloat16)
    bwd_out = bwd_out.reshape(sections, experts * TOK, D).astype(jnp.bfloat16)
    return fwd_out, bwd_out
```

```python
import jax
import jax.numpy as jnp
from jax import lax
from jax.sharding import PartitionSpec as P


def passed_along(block, axis, distance):
    devices = range(lax.axis_size(axis))
    route = [((i - distance) % len(devices), i) for i in devices]
    return lax.ppermute(block, axis, route)


def slot_table(route_rows, experts, capacity):
    flat_routes = route_rows.reshape(-1)
    matches = (flat_routes[:, None] == jnp.arange(experts, dtype=jnp.int32)[None, :]).astype(
        jnp.int32
    )
    before = jnp.cumsum(matches, axis=0) - matches
    slot_rank = jnp.sum(before * matches, axis=1)
    targets = flat_routes * capacity + slot_rank
    slot_ids = jnp.arange(experts * capacity, dtype=jnp.int32)
    return (targets[None, :] == slot_ids[:, None]).astype(jnp.bfloat16)


def silu_slope(pre_act):
    squash = jax.nn.sigmoid(pre_act)
    return squash * (1.0 + pre_act * (1.0 - squash))


def contract_last(left_rows, right_matrix):
    return lax.dot_general(
        left_rows, right_matrix, (((1,), (1,)), ((), ())), preferred_element_type=jnp.float32
    )


def matmul(left_rows, right_matrix):
    return jnp.dot(left_rows, right_matrix, preferred_element_type=jnp.float32)


def turned_parts(array, dim):
    parts = lax.axis_size("dp")
    own = lax.axis_index("dp")
    size = array.shape[dim] // parts
    return [
        lax.dynamic_slice_in_dim(array, lax.rem(own + j, parts) * size, size, axis=dim)
        for j in range(parts)
    ]


def summed_own(partials):
    total = partials[0]
    for j in range(1, len(partials)):
        total = total + passed_along(partials[j].astype(jnp.bfloat16), "dp", j).astype(jnp.float32)
    return total


def spread_own(block):
    others = [passed_along(block, "dp", -j) for j in range(1, lax.axis_size("dp"))]
    return jnp.concatenate([block] + others, axis=1)


def shards(
    fwd_act, fwd_routes, fwd_probs, bwd_grad, bwd_routes, bwd_probs, w_up, w_down, act_stash
):
    experts = lax.axis_size("expert")
    capacity = act_stash.shape[2] // experts
    top_count = fwd_routes.shape[2]
    arriving = passed_along(fwd_act[0], "section", 1)
    incoming = passed_along(bwd_grad[0], "section", -1)
    tokens_here = arriving.shape[0]
    width_part = arriving.shape[1]
    table_fwd = slot_table(fwd_routes[0], experts, capacity)
    table_bwd = slot_table(bwd_routes[0], experts, capacity)
    rows_fwd = jnp.repeat(arriving, top_count, axis=0)
    weighted = (bwd_probs[0][:, :, None] * incoming[:, None, :].astype(jnp.float32)).astype(
        jnp.bfloat16
    )
    weighted = weighted.reshape(tokens_here * top_count, width_part)
    sent_fwd = jnp.dot(table_fwd, rows_fwd, preferred_element_type=jnp.float32).astype(jnp.bfloat16)
    sent_bwd = jnp.dot(table_bwd, weighted, preferred_element_type=jnp.float32).astype(jnp.bfloat16)
    sent_fwd = sent_fwd.reshape(experts, capacity, width_part)
    sent_bwd = sent_bwd.reshape(experts, capacity, width_part)
    recv_fwd, recv_bwd = (
        lax.all_to_all(sent_fwd, "expert", split_axis=0, concat_axis=0, tiled=True),
        lax.all_to_all(sent_bwd, "expert", split_axis=0, concat_axis=0, tiled=True),
    )
    recv_fwd = recv_fwd.reshape(experts * capacity, width_part)
    recv_bwd = recv_bwd.reshape(experts * capacity, width_part)
    up_parts = turned_parts(w_up[0], 1)
    down_parts = turned_parts(w_down[0], 0)
    stash_own = turned_parts(act_stash[0, 0], 1)[0]
    slope_own = silu_slope(stash_own.astype(jnp.float32))
    pre_own = summed_own([matmul(recv_fwd, part) for part in up_parts])
    hidden_fwd = spread_own(jax.nn.silu(pre_own).astype(jnp.bfloat16))
    out_rows = matmul(hidden_fwd, jnp.concatenate(down_parts, axis=0)).astype(jnp.bfloat16)
    back_own = summed_own([contract_last(recv_bwd, part) for part in down_parts])
    grad_pre = spread_own((back_own * slope_own).astype(jnp.bfloat16))
    grad_rows = contract_last(grad_pre, jnp.concatenate(up_parts, axis=1)).astype(jnp.bfloat16)
    out_rows = out_rows.reshape(experts, capacity, width_part)
    grad_rows = grad_rows.reshape(experts, capacity, width_part)
    back_fwd, back_bwd = (
        lax.all_to_all(out_rows, "expert", split_axis=0, concat_axis=0, tiled=True),
        lax.all_to_all(grad_rows, "expert", split_axis=0, concat_axis=0, tiled=True),
    )
    back_fwd = back_fwd.reshape(experts * capacity, width_part)
    back_bwd = back_bwd.reshape(experts * capacity, width_part)
    picked_fwd = lax.dot_general(
        table_fwd, back_fwd, (((0,), (0,)), ((), ())), preferred_element_type=jnp.float32
    )
    picked_bwd = lax.dot_general(
        table_bwd, back_bwd, (((0,), (0,)), ((), ())), preferred_element_type=jnp.float32
    )
    picked_fwd = picked_fwd.reshape(tokens_here, top_count, width_part)
    picked_bwd = picked_bwd.reshape(tokens_here, top_count, width_part)
    fwd_out = jnp.sum(fwd_probs[0][:, :, None] * picked_fwd, axis=1).astype(jnp.bfloat16)
    bwd_out = jnp.sum(picked_bwd, axis=1).astype(jnp.bfloat16)
    return (fwd_out[None], bwd_out[None])


def solution(mesh):
    return jax.shard_map(
        shards,
        mesh=mesh,
        in_specs=(
            P("section", "expert", "dp"),
            P("section", "expert", None),
            P("section", "expert", None),
            P("section", "expert", "dp"),
            P("section", "expert", None),
            P("section", "expert", None),
            P("expert", "dp", None),
            P("expert", None, "dp"),
            P("section", "expert", None, None),
        ),
        out_specs=(P("section", "expert", "dp"), P("section", "expert", "dp")),
        check_vma=False,
    )
```

```python
import jax
import jax.numpy as jnp
from jax import lax
from jax.sharding import Mesh, PartitionSpec as P

ROWS = 4
CORES = 2
LANES = 128


def passed_along(block, axis, distance):
    devices = range(lax.axis_size(axis))
    route = [((i - distance) % len(devices), i) for i in devices]
    return lax.ppermute(block, axis, route)


def slot_targets(route_rows, experts, capacity):
    flat_routes = route_rows.reshape(-1)
    matches = (flat_routes[:, None] == jnp.arange(experts, dtype=jnp.int32)[None, :]).astype(
        jnp.int32
    )
    before = jnp.cumsum(matches, axis=0) - matches
    slot_rank = jnp.sum(before * matches, axis=1)
    return (flat_routes * capacity + slot_rank).reshape(route_rows.shape)


def silu_slope(pre_act):
    squash = jax.nn.sigmoid(pre_act)
    return squash * (1.0 + pre_act * (1.0 - squash))


def contract_last(left_rows, right_matrix):
    return lax.dot_general(
        left_rows, right_matrix, (((1,), (1,)), ((), ())), preferred_element_type=jnp.float32
    )


def contract_first(left_rows, right_rows):
    return lax.dot_general(
        left_rows, right_rows, (((0,), (0,)), ((), ())), preferred_element_type=jnp.float32
    )


def matmul(left_rows, right_matrix):
    return jnp.dot(left_rows, right_matrix, preferred_element_type=jnp.float32)


def bf16_pieces(values, count):
    pieces = []
    for _ in range(count):
        piece = lax.reduce_precision(values, 8, 7)
        pieces.append(piece.astype(jnp.bfloat16))
        values = values - piece
    return pieces


def turned_parts(array, dim):
    parts = lax.axis_size("dp")
    own = lax.axis_index("dp")
    size = array.shape[dim] // parts
    return [
        lax.dynamic_slice_in_dim(array, lax.rem(own + j, parts) * size, size, axis=dim)
        for j in range(parts)
    ]


def to_others(partials):
    return [
        passed_along(partials[j].astype(jnp.bfloat16), "dp", j) for j in range(1, len(partials))
    ]


def from_others(block):
    return [passed_along(block, "dp", -j) for j in range(1, lax.axis_size("dp"))]


def added(parts):
    total = parts[0].astype(jnp.float32)
    for part in parts[1:]:
        total = total + part.astype(jnp.float32)
    return total


def exchanged(rows, axes):
    size = lax.axis_size(axes)
    blocks = rows.reshape(size, rows.shape[0] // size, rows.shape[1])
    blocks = lax.all_to_all(blocks, axes, split_axis=0, concat_axis=0, tiled=True)
    return blocks.reshape(rows.shape)


def labels(targets, probs, pieces):
    fields = [targets.astype(jnp.bfloat16)] + bf16_pieces(probs, pieces)
    fields = jnp.concatenate(fields, axis=1)
    return jnp.pad(fields, ((0, 0), (0, LANES - fields.shape[1])))


def column_tokens(rows, label):
    message = jnp.concatenate([rows, label], axis=1)
    count = lax.axis_size("y")
    copies = jnp.broadcast_to(message[None], (count,) + message.shape)
    taken = lax.all_to_all(copies, "y", split_axis=0, concat_axis=0, tiled=True)
    taken = taken.reshape(count * message.shape[0], message.shape[1])
    return taken[:, : rows.shape[1]], taken[:, rows.shape[1] :].astype(jnp.float32)


def tables(label, top_count, capacity, pieces):
    columns, cores = lax.axis_size("y"), lax.axis_size("core")
    experts = lax.axis_size("x") * columns * cores
    tokens = label.shape[0] // columns
    slot = jnp.arange(experts * capacity, dtype=jnp.int32)
    place = slot % capacity
    group = (slot // capacity) % columns
    core = (slot // (capacity * columns)) % cores
    row = slot // (capacity * columns * cores)
    expert = (row * columns + lax.axis_index("y")) * cores + core
    wanted = expert * capacity + place + group * (experts * capacity)
    start = (jnp.arange(label.shape[0], dtype=jnp.int32) // tokens) * (experts * capacity)
    filled = jnp.zeros((label.shape[0], slot.shape[0]), jnp.bool_)
    probs = jnp.zeros(filled.shape, jnp.float32)
    for k in range(top_count):
        target = label[:, k].astype(jnp.int32) + start
        match = target[:, None] == wanted[None, :]
        filled = filled | match
        prob = label[:, top_count + k]
        for piece in range(1, pieces):
            prob = prob + label[:, (piece + 1) * top_count + k]
        probs = jnp.where(match, prob[:, None], probs)
    return filled.astype(jnp.bfloat16), probs


def shards(
    fwd_act, fwd_routes, fwd_probs, bwd_grad, bwd_routes, bwd_probs, w_up, w_down, act_stash
):
    columns = lax.axis_size("y")
    experts = lax.axis_size(("x", "y", "core"))
    capacity = act_stash.shape[2] // experts
    top_count = fwd_routes.shape[2]
    row_axes = ("x", "core")

    label_fwd = labels(slot_targets(fwd_routes[0], experts, capacity), fwd_probs[0], 2)
    arriving = passed_along(fwd_act[0], "section", 1)
    tokens_fwd, label_fwd = column_tokens(arriving, label_fwd)
    table_fwd, probs_fwd = tables(label_fwd, top_count, capacity, 2)
    sent_fwd = contract_first(table_fwd, tokens_fwd).astype(jnp.bfloat16)
    recv_fwd = exchanged(sent_fwd, row_axes)
    pick_fwd = jnp.concatenate(bf16_pieces(probs_fwd, 2), axis=0)

    grad_in, bwd_routes, arriving = lax.optimization_barrier((bwd_grad[0], bwd_routes, arriving))
    label_bwd = labels(slot_targets(bwd_routes[0], experts, capacity), bwd_probs[0], 3)
    incoming = passed_along(grad_in, "section", -1)
    up_parts = turned_parts(w_up[0], 1)
    down_parts = turned_parts(w_down[0], 0)
    stash = turned_parts(act_stash[0, 0], 1)[0]
    stash = stash.reshape(lax.axis_size("x"), columns, lax.axis_size("core"), capacity, -1)
    stash = stash.transpose(0, 2, 1, 3, 4).reshape(experts * capacity, -1)
    slope_own = silu_slope(stash.astype(jnp.float32))
    incoming, label_bwd, up_parts, down_parts, slope_own, recv_fwd = lax.optimization_barrier(
        (incoming, label_bwd, up_parts, down_parts, slope_own, recv_fwd)
    )
    tokens_bwd, label_bwd = column_tokens(incoming, label_bwd)
    table_bwd, probs_bwd = tables(label_bwd, top_count, capacity, 3)
    slot_prob = jnp.sum(probs_bwd, axis=0)
    sent_bwd = (slot_prob[:, None] * contract_first(table_bwd, tokens_bwd)).astype(jnp.bfloat16)
    recv_bwd = exchanged(sent_bwd, row_axes)

    pre_parts = [matmul(recv_fwd, part) for part in up_parts]
    pre_own = added([pre_parts[0]] + to_others(pre_parts))
    hidden_own = jax.nn.silu(pre_own).astype(jnp.bfloat16)
    hidden_fwd = jnp.concatenate([hidden_own] + from_others(hidden_own), axis=1)
    out_rows = matmul(hidden_fwd, jnp.concatenate(down_parts, axis=0)).astype(jnp.bfloat16)
    out_rows, recv_bwd = lax.optimization_barrier((out_rows, recv_bwd))
    back_fwd = exchanged(out_rows, row_axes)
    both = matmul(pick_fwd, back_fwd)
    half = both.shape[0] // 2
    part_fwd = (both[:half] + both[half:]).astype(jnp.bfloat16)

    def to_tokens(parts):
        parts = exchanged(parts, "y")
        size = parts.shape[0] // columns
        return added([parts[i * size : i * size + size] for i in range(columns)]).astype(
            jnp.bfloat16
        )

    fwd_out = to_tokens(part_fwd)

    back_parts = [contract_last(recv_bwd, part) for part in down_parts]
    back_own = added([back_parts[0]] + to_others(back_parts))
    grad_own = (back_own * slope_own).astype(jnp.bfloat16)
    grad_pre = jnp.concatenate([grad_own] + from_others(grad_own), axis=1)
    grad_rows = contract_last(grad_pre, jnp.concatenate(up_parts, axis=1)).astype(jnp.bfloat16)
    fwd_out, grad_rows = lax.optimization_barrier((fwd_out, grad_rows))
    back_bwd = exchanged(grad_rows, row_axes)
    part_bwd = matmul(table_bwd, back_bwd).astype(jnp.bfloat16)

    return (fwd_out[None], to_tokens(part_bwd)[None])


def solution(mesh):
    sections, experts, parts = mesh.devices.shape
    split = (sections, ROWS, experts // (ROWS * CORES), CORES, parts)
    mesh = Mesh(mesh.devices.reshape(split), ("section", "x", "y", "core", "dp"))
    expert = ("x", "y", "core")
    tokens = P("section", expert, "dp")
    routes = P("section", expert, None)
    return jax.shard_map(
        shards,
        mesh=mesh,
        in_specs=(
            tokens,
            routes,
            routes,
            tokens,
            routes,
            routes,
            P(expert, "dp", None),
            P(expert, None, "dp"),
            P("section", expert, None, None),
        ),
        out_specs=(tokens, tokens),
        check_vma=False,
    )
```

```python
import jax
import jax.numpy as jnp
from jax import lax
from jax.experimental import pallas as pl
from jax.experimental.pallas import tpu as pltpu
from jax.sharding import Mesh, PartitionSpec as P

CORES = 2
VMEM_LIMIT = 48 * 1024 * 1024


def passed_along(block, axis, distance):
    devices = range(lax.axis_size(axis))
    route = [((i - distance) % len(devices), i) for i in devices]
    return lax.ppermute(block, axis, route)


def slot_targets(route_rows, experts, capacity):
    flat_routes = route_rows.reshape(-1)
    matches = (flat_routes[:, None] == jnp.arange(experts, dtype=jnp.int32)[None, :]).astype(
        jnp.int32
    )
    before = jnp.cumsum(matches, axis=0) - matches
    slot_rank = jnp.sum(before * matches, axis=1)
    return (flat_routes * capacity + slot_rank).reshape(route_rows.shape)


def chip_tables(targets, probs, rows, capacity):
    tokens, top_count = targets.shape
    core = lax.axis_index("core")
    other = jnp.arange(tokens, dtype=jnp.int32) // (tokens // CORES)
    group_core = jnp.where(other == 0, core, 1 - core)
    expert, place = targets // capacity, targets % capacity
    here = expert % CORES == core
    row = ((expert // CORES) * CORES + group_core[:, None]) * capacity + place
    row = jnp.where(here, row, -1)
    slots = jnp.arange(rows, dtype=jnp.int32)[None, :]
    filled = jnp.zeros((tokens, rows), jnp.bool_)
    shares = jnp.zeros((tokens, rows), jnp.float32)
    for k in range(top_count):
        match = row[:, k : k + 1] == slots
        filled = filled | match
        shares = jnp.where(match, probs[:, k : k + 1], shares)
    return filled.astype(jnp.bfloat16), shares


def silu_slope(pre_act):
    squash = jax.nn.sigmoid(pre_act)
    return squash * (1.0 + pre_act * (1.0 - squash))


def contract_last(left_rows, right_matrix):
    return lax.dot_general(
        left_rows, right_matrix, (((1,), (1,)), ((), ())), preferred_element_type=jnp.float32
    )


def matmul(left_rows, right_matrix):
    return jnp.dot(left_rows, right_matrix, preferred_element_type=jnp.float32)


def turned_own(array):
    size = array.shape[1] // lax.axis_size("dp")
    return lax.dynamic_slice_in_dim(array, lax.axis_index("dp") * size, size, axis=1)


def block_spec(weight, dim, parts):
    shape = list(weight.shape)
    shape[dim] //= parts

    def place(j, own):
        turned = lax.rem(own[0] + j, parts)
        return (turned, 0) if dim == 0 else (0, turned)

    return pl.BlockSpec(tuple(shape), place)


def whole_spec(shape):
    return pl.BlockSpec(shape, lambda j, own: (0,) * len(shape))


def hidden_blocks(rows, weight, dim):
    parts = lax.axis_size("dp")
    size = weight.shape[dim] // parts
    block = (rows.shape[0], size)
    contract = (((1,), (1 - dim,)), ((), ()))

    def kernel(own, rows_ref, weight_ref, *out_refs):
        product = lax.dot_general(
            rows_ref[...], weight_ref[...], contract, preferred_element_type=jnp.float32
        )
        for k in range(parts):

            @pl.when(pl.program_id(0) == k)
            def _():
                out_refs[k][...] = product.astype(out_refs[k].dtype)

    kinds = [jnp.float32] + [jnp.bfloat16] * (parts - 1)
    results = pl.pallas_call(
        kernel,
        out_shape=[jax.ShapeDtypeStruct(block, kind) for kind in kinds],
        grid_spec=pltpu.PrefetchScalarGridSpec(
            num_scalar_prefetch=1,
            grid=(parts,),
            in_specs=[whole_spec(rows.shape), block_spec(weight, dim, parts)],
            out_specs=[whole_spec(block)] * parts,
        ),
        compiler_params=pltpu.CompilerParams(vmem_limit_bytes=VMEM_LIMIT),
    )(lax.axis_index("dp").reshape(1), rows, weight)
    return list(results)


def ranked_blocks(rows, weight):
    parts = lax.axis_size("dp")
    size = weight.shape[0] // parts
    block = (rows.shape[0], size)

    def kernel(own, rows_ref, weight_ref, own_ref, out_ref):
        product = contract_last(rows_ref[...], weight_ref[...])
        out_ref[0] = product.astype(out_ref.dtype)

        @pl.when(pl.program_id(0) == own[0])
        def _():
            own_ref[...] = product

    return pl.pallas_call(
        kernel,
        out_shape=[
            jax.ShapeDtypeStruct(block, jnp.float32),
            jax.ShapeDtypeStruct((parts,) + block, jnp.bfloat16),
        ],
        grid_spec=pltpu.PrefetchScalarGridSpec(
            num_scalar_prefetch=1,
            grid=(parts,),
            in_specs=[
                whole_spec(rows.shape),
                pl.BlockSpec((size, weight.shape[1]), lambda j, own: (j, 0)),
            ],
            out_specs=[whole_spec(block), pl.BlockSpec((1,) + block, lambda j, own: (j, 0, 0))],
        ),
        compiler_params=pltpu.CompilerParams(vmem_limit_bytes=VMEM_LIMIT),
    )(lax.axis_index("dp").reshape(1), rows, weight)


def model_rows(hidden_parts, weight, dim):
    parts = len(hidden_parts)
    out_shape = (hidden_parts[0].shape[0], weight.shape[1 - dim])
    contract = (((1,), (dim,)), ((), ()))

    def kernel(own, *refs):
        hidden_refs, (weight_ref, out_ref, total) = refs[:parts], refs[parts:]
        for k in range(parts):

            @pl.when(pl.program_id(0) == k)
            def _():
                product = lax.dot_general(
                    hidden_refs[k][...],
                    weight_ref[...],
                    contract,
                    preferred_element_type=jnp.float32,
                )
                if k == 0:
                    total[...] = product
                elif k < parts - 1:
                    total[...] += product
                else:
                    out_ref[...] = (total[...] + product).astype(out_ref.dtype)

    return pl.pallas_call(
        kernel,
        out_shape=jax.ShapeDtypeStruct(out_shape, jnp.bfloat16),
        grid_spec=pltpu.PrefetchScalarGridSpec(
            num_scalar_prefetch=1,
            grid=(parts,),
            in_specs=[whole_spec(part.shape) for part in hidden_parts]
            + [block_spec(weight, dim, parts)],
            out_specs=whole_spec(out_shape),
            scratch_shapes=[pltpu.VMEM(out_shape, jnp.float32)],
        ),
        compiler_params=pltpu.CompilerParams(vmem_limit_bytes=VMEM_LIMIT),
    )(lax.axis_index("dp").reshape(1), *hidden_parts, weight)


def summed_at_once(total, blocks):
    own = lax.axis_index("dp")
    blocks = lax.all_to_all(blocks, "dp", split_axis=0, concat_axis=0, tiled=True)
    for rank in range(blocks.shape[0]):
        total = total + jnp.where(own == rank, 0.0, blocks[rank].astype(jnp.float32))
    return total


def to_others(partials):
    return [
        passed_along(partials[j].astype(jnp.bfloat16), "dp", j) for j in range(1, len(partials))
    ]


def from_others(block):
    return [passed_along(block, "dp", -j) for j in range(1, lax.axis_size("dp"))]


def added(parts):
    total = parts[0]
    for part in parts[1:]:
        total = total + part.astype(jnp.float32)
    return total


def halves(values):
    coarse = lax.reduce_precision(values, 8, 7)
    return coarse.astype(jnp.bfloat16), (values - coarse).astype(jnp.bfloat16)


def contract_first(left_rows, right_rows):
    return lax.dot_general(
        left_rows, right_rows, (((0,), (0,)), ((), ())), preferred_element_type=jnp.float32
    )


def with_other_core(block):
    return jnp.concatenate([block, passed_along(block, "core", 1)], axis=0)


def shards(
    fwd_act, fwd_routes, fwd_probs, bwd_grad, bwd_routes, bwd_probs, w_up, w_down, act_stash
):
    chips = lax.axis_size("chip")
    experts = chips * lax.axis_size("core")
    tokens_here, width_part = fwd_act.shape[1:]
    rows = act_stash.shape[2]
    capacity = rows // experts

    def to_experts(block):
        block = block.reshape(chips, rows // chips, width_part)
        block = lax.all_to_all(block, "chip", split_axis=0, concat_axis=0, tiled=True)
        return block.reshape(rows, width_part)

    def to_tokens(part):
        other = passed_along(part[tokens_here:], "core", 1)
        return (part[:tokens_here] + other).astype(jnp.bfloat16)

    arriving = passed_along(fwd_act[0], "section", 1)
    targets = jnp.concatenate(
        [
            slot_targets(fwd_routes[0], experts, capacity),
            slot_targets(bwd_routes[0], experts, capacity),
        ],
        axis=1,
    )
    targets = with_other_core(targets)
    probs = with_other_core(jnp.concatenate([fwd_probs[0], bwd_probs[0]], axis=1))
    top_count = fwd_routes.shape[2]
    table_fwd, shares_fwd = chip_tables(
        targets[:, :top_count], probs[:, :top_count], rows, capacity
    )
    table_bwd, shares_bwd = chip_tables(
        targets[:, top_count:], probs[:, top_count:], rows, capacity
    )
    slot_probs = jnp.sum(shares_bwd, axis=0)[:, None]
    pick_fwd = jnp.concatenate(halves(shares_fwd), axis=0)

    sent_fwd = contract_first(table_fwd, with_other_core(arriving)).astype(jnp.bfloat16)
    sent_fwd, grad_in = lax.optimization_barrier((sent_fwd, bwd_grad[0]))
    recv_fwd = to_experts(sent_fwd)

    incoming = with_other_core(passed_along(grad_in, "section", -1))
    sent_bwd = (slot_probs * contract_first(table_bwd, incoming)).astype(jnp.bfloat16)
    stash_own = turned_own(act_stash[0, 0])
    slope_own = silu_slope(stash_own.astype(jnp.float32))
    sent_bwd, slope_own = lax.optimization_barrier((sent_bwd, slope_own))
    recv_bwd = to_experts(sent_bwd)

    up_weight, down_weight = w_up[0], w_down[0]
    pre_parts = hidden_blocks(recv_fwd, up_weight, 1)
    pre_own = added([pre_parts[0]] + to_others(pre_parts))
    hidden_own = jax.nn.silu(pre_own).astype(jnp.bfloat16)
    hidden_parts = [hidden_own] + from_others(hidden_own)
    hidden_parts[1], recv_bwd = lax.optimization_barrier((hidden_parts[1], recv_bwd))
    back_own = summed_at_once(*ranked_blocks(recv_bwd, down_weight))
    out_rows = model_rows(hidden_parts, down_weight, 0)
    out_rows, back_own = lax.optimization_barrier((out_rows, back_own))
    back_fwd = to_experts(out_rows)
    grad_own = (back_own * slope_own).astype(jnp.bfloat16)
    grad_rows = model_rows([grad_own] + from_others(grad_own), up_weight, 1)
    back_bwd = to_experts(grad_rows)

    both = matmul(pick_fwd, back_fwd)
    half = both.shape[0] // 2
    fwd_out = to_tokens(both[:half] + both[half:])
    bwd_out = to_tokens(matmul(table_bwd, back_bwd))
    return (fwd_out[None], bwd_out[None])


def solution(mesh):
    sections, experts, parts = mesh.devices.shape
    split = (sections, experts // CORES, CORES, parts)
    mesh = Mesh(mesh.devices.reshape(split), ("section", "chip", "core", "dp"))
    expert = ("chip", "core")
    tokens = P("section", expert, "dp")
    routes = P("section", expert, None)
    return jax.shard_map(
        shards,
        mesh=mesh,
        in_specs=(
            tokens,
            routes,
            routes,
            tokens,
            routes,
            routes,
            P(expert, "dp", None),
            P(expert, None, "dp"),
            P("section", expert, None, None),
        ),
        out_specs=(tokens, tokens),
        check_vma=False,
    )
```

```python
import jax
import jax.numpy as jnp
from jax import lax
from jax.experimental import pallas as pl
from jax.experimental.pallas import tpu as pltpu
from jax.sharding import Mesh, PartitionSpec as P

CORES = 2
VMEM_LIMIT = 48 * 1024 * 1024


def passed_along(block, axis, distance):
    devices = range(lax.axis_size(axis))
    route = [((i - distance) % len(devices), i) for i in devices]
    return lax.ppermute(block, axis, route)


def slot_targets(route_rows, experts, capacity):
    flat_routes = route_rows.reshape(-1)
    matches = (flat_routes[:, None] == jnp.arange(experts, dtype=jnp.int32)[None, :]).astype(
        jnp.int32
    )
    before = jnp.cumsum(matches, axis=0) - matches
    slot_rank = jnp.sum(before * matches, axis=1)
    return (flat_routes * capacity + slot_rank).reshape(route_rows.shape)


def chip_tables(targets, probs, rows, capacity):
    tokens, top_count = targets.shape
    core = lax.axis_index("core")
    other = jnp.arange(tokens, dtype=jnp.int32) // (tokens // CORES)
    group_core = jnp.where(other == 0, core, 1 - core)
    expert, place = targets // capacity, targets % capacity
    here = expert % CORES == core
    row = ((expert // CORES) * CORES + group_core[:, None]) * capacity + place
    row = jnp.where(here, row, -1)
    slots = jnp.arange(rows, dtype=jnp.int32)[None, :]
    filled = jnp.zeros((tokens, rows), jnp.bool_)
    shares = jnp.zeros((tokens, rows), jnp.float32)
    for k in range(top_count):
        match = row[:, k : k + 1] == slots
        filled = filled | match
        shares = jnp.where(match, probs[:, k : k + 1], shares)
    return filled.astype(jnp.bfloat16), shares


def silu_slope(pre_act):
    squash = jax.nn.sigmoid(pre_act)
    return squash * (1.0 + pre_act * (1.0 - squash))


def contract_last(left_rows, right_matrix):
    return lax.dot_general(
        left_rows, right_matrix, (((1,), (1,)), ((), ())), preferred_element_type=jnp.float32
    )


def matmul(left_rows, right_matrix):
    return jnp.dot(left_rows, right_matrix, preferred_element_type=jnp.float32)


def turned_own(array):
    size = array.shape[1] // lax.axis_size("dp")
    return lax.dynamic_slice_in_dim(array, lax.axis_index("dp") * size, size, axis=1)


def streamed(weight, dim, order, body, out_shape, inputs):
    parts = lax.axis_size("dp")
    size = weight.shape[dim] // parts
    shape = (size, weight.shape[1]) if dim == 0 else (weight.shape[0], size)

    def kernel(own, *refs):
        in_refs, weight_ref = refs[: len(inputs)], refs[len(inputs)]
        out_refs, blocks, arrived = refs[len(inputs) + 1 : -2], refs[-2], refs[-1]
        copies = []
        for j in range(parts):
            start = pl.multiple_of(order(own[0], j) * size, size)
            block = (
                weight_ref.at[pl.ds(start, size), :]
                if dim == 0
                else weight_ref.at[:, pl.ds(start, size)]
            )
            copies.append(pltpu.make_async_copy(block, blocks.at[j], arrived.at[j]))
            copies[j].start()
        carried = None
        for j in range(parts):
            copies[j].wait()
            carried = body(j, own[0], in_refs, blocks[j], out_refs, carried)

    return pl.pallas_call(
        kernel,
        out_shape=out_shape,
        in_specs=[pl.BlockSpec(memory_space=pltpu.SMEM)]
        + [pl.BlockSpec(memory_space=pltpu.VMEM)] * len(inputs)
        + [pl.BlockSpec(memory_space=pltpu.HBM)],
        out_specs=jax.tree.map(lambda _: pl.BlockSpec(memory_space=pltpu.VMEM), out_shape),
        scratch_shapes=[
            pltpu.VMEM((parts,) + shape, weight.dtype),
            pltpu.SemaphoreType.DMA((parts,)),
        ],
        compiler_params=pltpu.CompilerParams(vmem_limit_bytes=VMEM_LIMIT),
    )(lax.axis_index("dp").reshape(1), *inputs, pltpu.with_memory_space_constraint(weight, pltpu.HBM))


def turned(own, j):
    return lax.rem(own + j, lax.axis_size("dp"))


def product(left, right, dim):
    return lax.dot_general(
        left, right, (((1,), (dim,)), ((), ())), preferred_element_type=jnp.float32
    )


def hidden_blocks(rows, weight, dim):
    parts = lax.axis_size("dp")
    block = (rows.shape[0], weight.shape[dim] // parts)

    def body(j, own, in_refs, weight_block, out_refs, carried):
        out_refs[j][...] = product(in_refs[0][...], weight_block, 1 - dim).astype(
            out_refs[j].dtype
        )

    kinds = [jnp.float32] + [jnp.bfloat16] * (parts - 1)
    out_shape = [jax.ShapeDtypeStruct(block, kind) for kind in kinds]
    return list(streamed(weight, dim, turned, body, out_shape, [rows]))


def ranked_blocks(rows, weight):
    parts = lax.axis_size("dp")
    block = (rows.shape[0], weight.shape[0] // parts)

    def body(j, own, in_refs, weight_block, out_refs, carried):
        result = product(in_refs[0][...], weight_block, 1)
        out_refs[1][j] = result.astype(jnp.bfloat16)

        @pl.when(own == j)
        def _():
            out_refs[0][...] = result

    out_shape = [
        jax.ShapeDtypeStruct(block, jnp.float32),
        jax.ShapeDtypeStruct((parts,) + block, jnp.bfloat16),
    ]
    return streamed(weight, 0, lambda own, j: j, body, out_shape, [rows])


def model_rows(hidden_parts, weight, dim):
    parts = len(hidden_parts)
    out_shape = (hidden_parts[0].shape[0], weight.shape[1 - dim])

    def body(j, own, in_refs, weight_block, out_refs, carried):
        result = product(in_refs[j][...], weight_block, dim)
        total = result if carried is None else carried + result
        if j == parts - 1:
            out_refs[0][...] = total.astype(jnp.bfloat16)
        return total

    out_shape = jax.ShapeDtypeStruct(out_shape, jnp.bfloat16)
    return streamed(weight, dim, turned, body, out_shape, hidden_parts)


def summed_at_once(total, blocks):
    own = lax.axis_index("dp")
    blocks = lax.all_to_all(blocks, "dp", split_axis=0, concat_axis=0, tiled=True)
    for rank in range(blocks.shape[0]):
        total = total + jnp.where(own == rank, 0.0, blocks[rank].astype(jnp.float32))
    return total


def to_others(partials):
    return [
        passed_along(partials[j].astype(jnp.bfloat16), "dp", j) for j in range(1, len(partials))
    ]


def from_others(block):
    return [passed_along(block, "dp", -j) for j in range(1, lax.axis_size("dp"))]


def added(parts):
    total = parts[0]
    for part in parts[1:]:
        total = total + part.astype(jnp.float32)
    return total


def halves(values):
    coarse = lax.reduce_precision(values, 8, 7)
    return coarse.astype(jnp.bfloat16), (values - coarse).astype(jnp.bfloat16)


def contract_first(left_rows, right_rows):
    return lax.dot_general(
        left_rows, right_rows, (((0,), (0,)), ((), ())), preferred_element_type=jnp.float32
    )


def with_other_core(block):
    return jnp.concatenate([block, passed_along(block, "core", 1)], axis=0)


def shards(
    fwd_act, fwd_routes, fwd_probs, bwd_grad, bwd_routes, bwd_probs, w_up, w_down, act_stash
):
    chips = lax.axis_size("chip")
    experts = chips * lax.axis_size("core")
    tokens_here, width_part = fwd_act.shape[1:]
    rows = act_stash.shape[2]
    capacity = rows // experts

    def to_experts(block):
        block = block.reshape(chips, rows // chips, width_part)
        block = lax.all_to_all(block, "chip", split_axis=0, concat_axis=0, tiled=True)
        return block.reshape(rows, width_part)

    def to_tokens(part):
        other = passed_along(part[tokens_here:], "core", 1)
        return (part[:tokens_here] + other).astype(jnp.bfloat16)

    arriving = passed_along(fwd_act[0], "section", 1)
    targets = jnp.concatenate(
        [
            slot_targets(fwd_routes[0], experts, capacity),
            slot_targets(bwd_routes[0], experts, capacity),
        ],
        axis=1,
    )
    targets = with_other_core(targets)
    probs = with_other_core(jnp.concatenate([fwd_probs[0], bwd_probs[0]], axis=1))
    top_count = fwd_routes.shape[2]
    table_fwd, shares_fwd = chip_tables(
        targets[:, :top_count], probs[:, :top_count], rows, capacity
    )
    table_bwd, shares_bwd = chip_tables(
        targets[:, top_count:], probs[:, top_count:], rows, capacity
    )
    slot_probs = jnp.sum(shares_bwd, axis=0)[:, None]
    pick_fwd = jnp.concatenate(halves(shares_fwd), axis=0)

    sent_fwd = contract_first(table_fwd, with_other_core(arriving)).astype(jnp.bfloat16)
    sent_fwd, grad_in = lax.optimization_barrier((sent_fwd, bwd_grad[0]))
    recv_fwd = to_experts(sent_fwd)

    incoming = with_other_core(passed_along(grad_in, "section", -1))
    sent_bwd = (slot_probs * contract_first(table_bwd, incoming)).astype(jnp.bfloat16)
    stash_own = turned_own(act_stash[0, 0])
    slope_own = silu_slope(stash_own.astype(jnp.float32))
    sent_bwd, slope_own = lax.optimization_barrier((sent_bwd, slope_own))
    recv_bwd = to_experts(sent_bwd)

    up_weight, down_weight = w_up[0], w_down[0]
    pre_parts = hidden_blocks(recv_fwd, up_weight, 1)
    pre_own = added([pre_parts[0]] + to_others(pre_parts))
    hidden_own = jax.nn.silu(pre_own).astype(jnp.bfloat16)
    hidden_own, recv_bwd = lax.optimization_barrier((hidden_own, recv_bwd))
    hidden_parts = [hidden_own] + from_others(hidden_own)
    back_parts = hidden_blocks(recv_bwd, down_weight, 0)
    back_parts = [back_parts[0]] + to_others(back_parts)
    out_rows = model_rows(hidden_parts, down_weight, 0)
    out_rows, back_parts = lax.optimization_barrier((out_rows, back_parts))
    back_own = added(back_parts)
    back_fwd = to_experts(out_rows)
    grad_own = (back_own * slope_own).astype(jnp.bfloat16)
    grad_rows = model_rows([grad_own] + from_others(grad_own), up_weight, 1)
    back_bwd = to_experts(grad_rows)

    both = matmul(pick_fwd, back_fwd)
    half = both.shape[0] // 2
    fwd_out = to_tokens(both[:half] + both[half:])
    bwd_out = to_tokens(matmul(table_bwd, back_bwd))
    return (fwd_out[None], bwd_out[None])


def solution(mesh):
    sections, experts, parts = mesh.devices.shape
    split = (sections, experts // CORES, CORES, parts)
    mesh = Mesh(mesh.devices.reshape(split), ("section", "chip", "core", "dp"))
    expert = ("chip", "core")
    tokens = P("section", expert, "dp")
    routes = P("section", expert, None)
    return jax.shard_map(
        shards,
        mesh=mesh,
        in_specs=(
            tokens,
            routes,
            routes,
            tokens,
            routes,
            routes,
            P(expert, "dp", None),
            P(expert, None, "dp"),
            P("section", expert, None, None),
        ),
        out_specs=(tokens, tokens),
        check_vma=False,
    )
```

```python
import jax
import jax.numpy as jnp
from jax import lax
from jax.experimental import pallas as pl
from jax.experimental.pallas import tpu as pltpu
from jax.sharding import Mesh, PartitionSpec as P

CORES = 2
LANES = 128
VMEM_LIMIT = 48 * 1024 * 1024


def passed_along(block, axis, distance):
    devices = range(lax.axis_size(axis))
    route = [((i - distance) % len(devices), i) for i in devices]
    return lax.ppermute(block, axis, route)


def slot_targets(route_rows, experts, capacity):
    flat_routes = route_rows.reshape(-1)
    matches = (flat_routes[:, None] == jnp.arange(experts, dtype=jnp.int32)[None, :]).astype(
        jnp.int32
    )
    before = jnp.cumsum(matches, axis=0) - matches
    slot_rank = jnp.sum(before * matches, axis=1)
    return (flat_routes * capacity + slot_rank).reshape(route_rows.shape)


def chip_tables(targets, probs, rows, capacity):
    tokens, top_count = targets.shape
    core = lax.axis_index("core")
    other = jnp.arange(tokens, dtype=jnp.int32) // (tokens // CORES)
    group_core = jnp.where(other == 0, core, 1 - core)
    expert, place = targets // capacity, targets % capacity
    here = expert % CORES == core
    row = ((expert // CORES) * CORES + group_core[:, None]) * capacity + place
    row = jnp.where(here, row, -1)
    slots = jnp.arange(rows, dtype=jnp.int32)[None, :]
    filled = jnp.zeros((tokens, rows), jnp.bool_)
    shares = jnp.zeros((tokens, rows), jnp.float32)
    for k in range(top_count):
        match = row[:, k : k + 1] == slots
        filled = filled | match
        shares = jnp.where(match, probs[:, k : k + 1], shares)
    return filled.astype(jnp.bfloat16), shares


def silu_slope(pre_act):
    squash = jax.nn.sigmoid(pre_act)
    return squash * (1.0 + pre_act * (1.0 - squash))


def contract_last(left_rows, right_matrix):
    return lax.dot_general(
        left_rows, right_matrix, (((1,), (1,)), ((), ())), preferred_element_type=jnp.float32
    )


def matmul(left_rows, right_matrix):
    return jnp.dot(left_rows, right_matrix, preferred_element_type=jnp.float32)


def turned_own(array):
    size = array.shape[1] // lax.axis_size("dp")
    return lax.dynamic_slice_in_dim(array, lax.axis_index("dp") * size, size, axis=1)


def streamed(weight, dim, order, body, out_shape, inputs):
    parts = lax.axis_size("dp")
    size = weight.shape[dim] // parts
    shape = (size, weight.shape[1]) if dim == 0 else (weight.shape[0], size)

    def kernel(own, *refs):
        in_refs, weight_ref = refs[: len(inputs)], refs[len(inputs)]
        out_refs, blocks, arrived = refs[len(inputs) + 1 : -2], refs[-2], refs[-1]
        copies = []
        for j in range(parts):
            start = pl.multiple_of(order(own[0], j) * size, size)
            block = (
                weight_ref.at[pl.ds(start, size), :]
                if dim == 0
                else weight_ref.at[:, pl.ds(start, size)]
            )
            copies.append(pltpu.make_async_copy(block, blocks.at[j], arrived.at[j]))
            copies[j].start()
        carried = None
        for j in range(parts):
            copies[j].wait()
            carried = body(j, own[0], in_refs, blocks[j], out_refs, carried)

    return pl.pallas_call(
        kernel,
        out_shape=out_shape,
        in_specs=[pl.BlockSpec(memory_space=pltpu.SMEM)]
        + [pl.BlockSpec(memory_space=pltpu.VMEM)] * len(inputs)
        + [pl.BlockSpec(memory_space=pltpu.HBM)],
        out_specs=jax.tree.map(lambda _: pl.BlockSpec(memory_space=pltpu.VMEM), out_shape),
        scratch_shapes=[
            pltpu.VMEM((parts,) + shape, weight.dtype),
            pltpu.SemaphoreType.DMA((parts,)),
        ],
        compiler_params=pltpu.CompilerParams(vmem_limit_bytes=VMEM_LIMIT),
    )(lax.axis_index("dp").reshape(1), *inputs, pltpu.with_memory_space_constraint(weight, pltpu.HBM))


def turned(own, j):
    return lax.rem(own + j, lax.axis_size("dp"))


def product(left, right, dim):
    return lax.dot_general(
        left, right, (((1,), (dim,)), ((), ())), preferred_element_type=jnp.float32
    )


def hidden_blocks(rows, weight, dim):
    parts = lax.axis_size("dp")
    block = (rows.shape[0], weight.shape[dim] // parts)

    def body(j, own, in_refs, weight_block, out_refs, carried):
        out_refs[j][...] = product(in_refs[0][...], weight_block, 1 - dim).astype(
            out_refs[j].dtype
        )

    kinds = [jnp.float32] + [jnp.bfloat16] * (parts - 1)
    out_shape = [jax.ShapeDtypeStruct(block, kind) for kind in kinds]
    return list(streamed(weight, dim, turned, body, out_shape, [rows]))


def ranked_blocks(rows, weight):
    parts = lax.axis_size("dp")
    block = (rows.shape[0], weight.shape[0] // parts)

    def body(j, own, in_refs, weight_block, out_refs, carried):
        result = product(in_refs[0][...], weight_block, 1)
        out_refs[1][j] = result.astype(jnp.bfloat16)

        @pl.when(own == j)
        def _():
            out_refs[0][...] = result

    out_shape = [
        jax.ShapeDtypeStruct(block, jnp.float32),
        jax.ShapeDtypeStruct((parts,) + block, jnp.bfloat16),
    ]
    return streamed(weight, 0, lambda own, j: j, body, out_shape, [rows])


def model_rows(hidden_parts, weight, dim):
    parts = len(hidden_parts)
    out_shape = (hidden_parts[0].shape[0], weight.shape[1 - dim])

    def body(j, own, in_refs, weight_block, out_refs, carried):
        result = product(in_refs[j][...], weight_block, dim)
        total = result if carried is None else carried + result
        if j == parts - 1:
            out_refs[0][...] = total.astype(jnp.bfloat16)
        return total

    out_shape = jax.ShapeDtypeStruct(out_shape, jnp.bfloat16)
    return streamed(weight, dim, turned, body, out_shape, hidden_parts)


def summed_at_once(total, blocks):
    own = lax.axis_index("dp")
    blocks = lax.all_to_all(blocks, "dp", split_axis=0, concat_axis=0, tiled=True)
    for rank in range(blocks.shape[0]):
        total = total + jnp.where(own == rank, 0.0, blocks[rank].astype(jnp.float32))
    return total


def to_others(partials):
    return [
        passed_along(partials[j].astype(jnp.bfloat16), "dp", j) for j in range(1, len(partials))
    ]


def from_others(block):
    return [passed_along(block, "dp", -j) for j in range(1, lax.axis_size("dp"))]


def added(parts):
    total = parts[0]
    for part in parts[1:]:
        total = total + part.astype(jnp.float32)
    return total


def halves(values):
    coarse = lax.reduce_precision(values, 8, 7)
    return coarse.astype(jnp.bfloat16), (values - coarse).astype(jnp.bfloat16)


def contract_first(left_rows, right_rows):
    return lax.dot_general(
        left_rows, right_rows, (((0,), (0,)), ((), ())), preferred_element_type=jnp.float32
    )


def labels(targets, probs, pieces):
    fields = [targets.astype(jnp.bfloat16)]
    for _ in range(pieces):
        piece = lax.reduce_precision(probs, 8, 7)
        fields.append(piece.astype(jnp.bfloat16))
        probs = probs - piece
    fields = jnp.concatenate(fields, axis=1)
    return jnp.pad(fields, ((0, 0), (0, LANES - fields.shape[1])))


def with_other_core(rows, label, top_count, pieces):
    message = jnp.concatenate([rows, label], axis=1)
    other = passed_along(message, "core", 1)
    width = rows.shape[1]
    both = jnp.concatenate([rows, other[:, :width]], axis=0)
    label = jnp.concatenate([label, other[:, width:]], axis=0).astype(jnp.float32)
    targets = label[:, :top_count].astype(jnp.int32)
    probs = label[:, top_count : 2 * top_count]
    for k in range(2, pieces + 1):
        probs = probs + label[:, k * top_count : (k + 1) * top_count]
    return both, targets, probs


def shards(
    fwd_act, fwd_routes, fwd_probs, bwd_grad, bwd_routes, bwd_probs, w_up, w_down, act_stash
):
    chips = lax.axis_size("chip")
    experts = chips * lax.axis_size("core")
    tokens_here, width_part = fwd_act.shape[1:]
    rows = act_stash.shape[2]
    capacity = rows // experts

    def to_experts(block):
        block = block.reshape(chips, rows // chips, width_part)
        block = lax.all_to_all(block, "chip", split_axis=0, concat_axis=0, tiled=True)
        return block.reshape(rows, width_part)

    def to_tokens(part):
        other = passed_along(part[tokens_here:], "core", 1)
        return (part[:tokens_here] + other).astype(jnp.bfloat16)

    arriving = passed_along(fwd_act[0], "section", 1)
    top_count = fwd_routes.shape[2]
    label_fwd = labels(slot_targets(fwd_routes[0], experts, capacity), fwd_probs[0], 2)
    tokens_fwd, targets_fwd, probs_fwd = with_other_core(arriving, label_fwd, top_count, 2)
    table_fwd, shares_fwd = chip_tables(targets_fwd, probs_fwd, rows, capacity)
    pick_fwd = jnp.concatenate(halves(shares_fwd), axis=0)

    sent_fwd = contract_first(table_fwd, tokens_fwd).astype(jnp.bfloat16)
    sent_fwd, grad_in = lax.optimization_barrier((sent_fwd, bwd_grad[0]))
    recv_fwd = to_experts(sent_fwd)

    label_bwd = labels(slot_targets(bwd_routes[0], experts, capacity), bwd_probs[0], 3)
    incoming = passed_along(grad_in, "section", -1)
    incoming, targets_bwd, probs_bwd = with_other_core(incoming, label_bwd, top_count, 3)
    table_bwd, shares_bwd = chip_tables(targets_bwd, probs_bwd, rows, capacity)
    slot_probs = jnp.sum(shares_bwd, axis=0)[:, None]
    sent_bwd = (slot_probs * contract_first(table_bwd, incoming)).astype(jnp.bfloat16)
    stash_own = turned_own(act_stash[0, 0])
    slope_own = silu_slope(stash_own.astype(jnp.float32))
    sent_bwd, slope_own = lax.optimization_barrier((sent_bwd, slope_own))
    recv_bwd = to_experts(sent_bwd)

    up_weight, down_weight = w_up[0], w_down[0]
    pre_parts = hidden_blocks(recv_fwd, up_weight, 1)
    pre_own = added([pre_parts[0]] + to_others(pre_parts))
    hidden_own = jax.nn.silu(pre_own).astype(jnp.bfloat16)
    hidden_own, recv_bwd = lax.optimization_barrier((hidden_own, recv_bwd))
    hidden_parts = [hidden_own] + from_others(hidden_own)
    back_parts = hidden_blocks(recv_bwd, down_weight, 0)
    back_parts = [back_parts[0]] + to_others(back_parts)
    out_rows = model_rows(hidden_parts, down_weight, 0)
    out_rows, back_parts = lax.optimization_barrier((out_rows, back_parts))
    back_own = added(back_parts)
    back_fwd = to_experts(out_rows)
    grad_own = (back_own * slope_own).astype(jnp.bfloat16)
    grad_rows = model_rows([grad_own] + from_others(grad_own), up_weight, 1)
    back_bwd = to_experts(grad_rows)

    both = matmul(pick_fwd, back_fwd)
    half = both.shape[0] // 2
    fwd_out = to_tokens(both[:half] + both[half:])
    bwd_out = to_tokens(matmul(table_bwd, back_bwd))
    return (fwd_out[None], bwd_out[None])


def solution(mesh):
    sections, experts, parts = mesh.devices.shape
    split = (sections, experts // CORES, CORES, parts)
    mesh = Mesh(mesh.devices.reshape(split), ("section", "chip", "core", "dp"))
    expert = ("chip", "core")
    tokens = P("section", expert, "dp")
    routes = P("section", expert, None)
    return jax.shard_map(
        shards,
        mesh=mesh,
        in_specs=(
            tokens,
            routes,
            routes,
            tokens,
            routes,
            routes,
            P(expert, "dp", None),
            P(expert, None, "dp"),
            P("section", expert, None, None),
        ),
        out_specs=(tokens, tokens),
        check_vma=False,
    )
```

```python
import jax
import jax.numpy as jnp
from jax import lax
from jax.experimental import pallas as pl
from jax.experimental.pallas import tpu as pltpu
from jax.sharding import Mesh, PartitionSpec as P

CORES = 2
LANES = 128
VMEM_LIMIT = 48 * 1024 * 1024


def passed_along(block, axis, distance):
    devices = range(lax.axis_size(axis))
    route = [((i - distance) % len(devices), i) for i in devices]
    return lax.ppermute(block, axis, route)


def slot_targets(route_rows, experts, capacity):
    flat_routes = route_rows.reshape(-1)
    matches = (flat_routes[:, None] == jnp.arange(experts, dtype=jnp.int32)[None, :]).astype(
        jnp.int32
    )
    before = jnp.cumsum(matches, axis=0) - matches
    slot_rank = jnp.sum(before * matches, axis=1)
    return (flat_routes * capacity + slot_rank).reshape(route_rows.shape)


def chip_tables(targets, probs, rows, capacity):
    tokens, top_count = targets.shape
    core = lax.axis_index("core")
    other = jnp.arange(tokens, dtype=jnp.int32) // (tokens // CORES)
    group_core = jnp.where(other == 0, core, 1 - core)
    expert, place = targets // capacity, targets % capacity
    here = expert % CORES == core
    row = ((expert // CORES) * CORES + group_core[:, None]) * capacity + place
    row = jnp.where(here, row, -1)
    slots = jnp.arange(rows, dtype=jnp.int32)[None, :]
    filled = jnp.zeros((tokens, rows), jnp.bool_)
    shares = jnp.zeros((tokens, rows), jnp.float32)
    for k in range(top_count):
        match = row[:, k : k + 1] == slots
        filled = filled | match
        shares = jnp.where(match, probs[:, k : k + 1], shares)
    return filled.astype(jnp.bfloat16), shares


def silu_slope(pre_act):
    squash = jax.nn.sigmoid(pre_act)
    return squash * (1.0 + pre_act * (1.0 - squash))


def contract_last(left_rows, right_matrix):
    return lax.dot_general(
        left_rows, right_matrix, (((1,), (1,)), ((), ())), preferred_element_type=jnp.float32
    )


def matmul(left_rows, right_matrix):
    return jnp.dot(left_rows, right_matrix, preferred_element_type=jnp.float32)


def turned_own(array):
    size = array.shape[1] // lax.axis_size("dp")
    return lax.dynamic_slice_in_dim(array, lax.axis_index("dp") * size, size, axis=1)


def streamed(weight, dim, order, body, out_shape, inputs):
    parts = lax.axis_size("dp")
    size = weight.shape[dim] // parts
    shape = (size, weight.shape[1]) if dim == 0 else (weight.shape[0], size)

    def kernel(own, *refs):
        in_refs, weight_ref = refs[: len(inputs)], refs[len(inputs)]
        out_refs, blocks, arrived = refs[len(inputs) + 1 : -2], refs[-2], refs[-1]
        copies = []
        for j in range(parts):
            start = pl.multiple_of(order(own[0], j) * size, size)
            block = (
                weight_ref.at[pl.ds(start, size), :]
                if dim == 0
                else weight_ref.at[:, pl.ds(start, size)]
            )
            copies.append(pltpu.make_async_copy(block, blocks.at[j], arrived.at[j]))
            copies[j].start()
        carried = None
        for j in range(parts):
            copies[j].wait()
            carried = body(j, own[0], in_refs, blocks[j], out_refs, carried)

    return pl.pallas_call(
        kernel,
        out_shape=out_shape,
        in_specs=[pl.BlockSpec(memory_space=pltpu.SMEM)]
        + [pl.BlockSpec(memory_space=pltpu.VMEM)] * len(inputs)
        + [pl.BlockSpec(memory_space=pltpu.HBM)],
        out_specs=jax.tree.map(lambda _: pl.BlockSpec(memory_space=pltpu.VMEM), out_shape),
        scratch_shapes=[
            pltpu.VMEM((parts,) + shape, weight.dtype),
            pltpu.SemaphoreType.DMA((parts,)),
        ],
        compiler_params=pltpu.CompilerParams(vmem_limit_bytes=VMEM_LIMIT),
    )(lax.axis_index("dp").reshape(1), *inputs, pltpu.with_memory_space_constraint(weight, pltpu.HBM))


def turned(own, j):
    return lax.rem(own + j, lax.axis_size("dp"))


def product(left, right, dim):
    return lax.dot_general(
        left, right, (((1,), (dim,)), ((), ())), preferred_element_type=jnp.float32
    )


def hidden_blocks(rows, weight, dim):
    parts = lax.axis_size("dp")
    block = (rows.shape[0], weight.shape[dim] // parts)

    def body(j, own, in_refs, weight_block, out_refs, carried):
        out_refs[j][...] = product(in_refs[0][...], weight_block, 1 - dim).astype(
            out_refs[j].dtype
        )

    kinds = [jnp.float32] + [jnp.bfloat16] * (parts - 1)
    out_shape = [jax.ShapeDtypeStruct(block, kind) for kind in kinds]
    return list(streamed(weight, dim, turned, body, out_shape, [rows]))


def ranked_blocks(rows, weight):
    parts = lax.axis_size("dp")
    block = (rows.shape[0], weight.shape[0] // parts)

    def body(j, own, in_refs, weight_block, out_refs, carried):
        result = product(in_refs[0][...], weight_block, 1)
        out_refs[1][j] = result.astype(jnp.bfloat16)

        @pl.when(own == j)
        def _():
            out_refs[0][...] = result

    out_shape = [
        jax.ShapeDtypeStruct(block, jnp.float32),
        jax.ShapeDtypeStruct((parts,) + block, jnp.bfloat16),
    ]
    return streamed(weight, 0, lambda own, j: j, body, out_shape, [rows])


def model_rows(hidden_parts, weight, dim):
    parts = len(hidden_parts)
    out_shape = (hidden_parts[0].shape[0], weight.shape[1 - dim])

    def body(j, own, in_refs, weight_block, out_refs, carried):
        result = product(in_refs[j][...], weight_block, dim)
        total = result if carried is None else carried + result
        if j == parts - 1:
            out_refs[0][...] = total.astype(jnp.bfloat16)
        return total

    out_shape = jax.ShapeDtypeStruct(out_shape, jnp.bfloat16)
    return streamed(weight, dim, turned, body, out_shape, hidden_parts)


def summed_at_once(total, blocks):
    own = lax.axis_index("dp")
    blocks = lax.all_to_all(blocks, "dp", split_axis=0, concat_axis=0, tiled=True)
    for rank in range(blocks.shape[0]):
        total = total + jnp.where(own == rank, 0.0, blocks[rank].astype(jnp.float32))
    return total


def to_others(partials):
    return [
        passed_along(partials[j].astype(jnp.bfloat16), "dp", j) for j in range(1, len(partials))
    ]


def from_others(block):
    return [passed_along(block, "dp", -j) for j in range(1, lax.axis_size("dp"))]


def added(parts):
    total = parts[0]
    for part in parts[1:]:
        total = total + part.astype(jnp.float32)
    return total


def halves(values):
    coarse = lax.reduce_precision(values, 8, 7)
    return coarse.astype(jnp.bfloat16), (values - coarse).astype(jnp.bfloat16)


def contract_first(left_rows, right_rows):
    return lax.dot_general(
        left_rows, right_rows, (((0,), (0,)), ((), ())), preferred_element_type=jnp.float32
    )


def labels(targets, probs, pieces):
    fields = [targets.astype(jnp.bfloat16)]
    for _ in range(pieces):
        piece = lax.reduce_precision(probs, 8, 7)
        fields.append(piece.astype(jnp.bfloat16))
        probs = probs - piece
    fields = jnp.concatenate(fields, axis=1)
    return jnp.pad(fields, ((0, 0), (0, LANES - fields.shape[1])))


def with_other_core(rows, label, top_count, pieces):
    message = jnp.concatenate([rows, label], axis=1)
    other = passed_along(message, "core", 1)
    width = rows.shape[1]
    both = jnp.concatenate([rows, other[:, :width]], axis=0)
    label = jnp.concatenate([label, other[:, width:]], axis=0).astype(jnp.float32)
    targets = label[:, :top_count].astype(jnp.int32)
    probs = label[:, top_count : 2 * top_count]
    for k in range(2, pieces + 1):
        probs = probs + label[:, k * top_count : (k + 1) * top_count]
    return both, targets, probs


def shards(
    fwd_act, fwd_routes, fwd_probs, bwd_grad, bwd_routes, bwd_probs, w_up, w_down, act_stash
):
    chips = lax.axis_size("chip")
    experts = chips * lax.axis_size("core")
    tokens_here, width_part = fwd_act.shape[1:]
    rows = act_stash.shape[2]
    capacity = rows // experts

    def to_experts(block):
        block = block.reshape(chips, rows // chips, width_part)
        block = lax.all_to_all(block, "chip", split_axis=0, concat_axis=0, tiled=True)
        return block.reshape(rows, width_part)

    def to_tokens(part):
        other = passed_along(part[tokens_here:], "core", 1)
        return (part[:tokens_here] + other).astype(jnp.bfloat16)

    arriving = passed_along(fwd_act[0], "section", 1)
    top_count = fwd_routes.shape[2]
    label_fwd = labels(slot_targets(fwd_routes[0], experts, capacity), fwd_probs[0], 2)
    tokens_fwd, targets_fwd, probs_fwd = with_other_core(arriving, label_fwd, top_count, 2)
    table_fwd, shares_fwd = chip_tables(targets_fwd, probs_fwd, rows, capacity)
    pick_fwd = jnp.concatenate(halves(shares_fwd), axis=0)

    sent_fwd = contract_first(table_fwd, tokens_fwd).astype(jnp.bfloat16)
    sent_fwd, grad_in = lax.optimization_barrier((sent_fwd, bwd_grad[0]))
    recv_fwd = to_experts(sent_fwd)

    label_bwd = labels(slot_targets(bwd_routes[0], experts, capacity), bwd_probs[0], 3)
    incoming = passed_along(grad_in, "section", -1)
    incoming, targets_bwd, probs_bwd = with_other_core(incoming, label_bwd, top_count, 3)
    table_bwd, shares_bwd = chip_tables(targets_bwd, probs_bwd, rows, capacity)
    slot_probs = jnp.sum(shares_bwd, axis=0)[:, None]
    sent_bwd = (slot_probs * contract_first(table_bwd, incoming)).astype(jnp.bfloat16)
    stash_own = turned_own(act_stash[0, 0])
    slope_own = silu_slope(stash_own.astype(jnp.float32))
    sent_bwd, slope_own = lax.optimization_barrier((sent_bwd, slope_own))
    recv_bwd = to_experts(sent_bwd)

    up_weight, down_weight = w_up[0], w_down[0]
    pre_parts = hidden_blocks(recv_fwd, up_weight, 1)
    pre_own = added([pre_parts[0]] + to_others(pre_parts))
    hidden_own = jax.nn.silu(pre_own).astype(jnp.bfloat16)
    hidden_parts = [hidden_own] + from_others(hidden_own)
    hidden_parts[2], recv_bwd = lax.optimization_barrier((hidden_parts[2], recv_bwd))
    back_parts = hidden_blocks(recv_bwd, down_weight, 0)
    back_parts = [back_parts[0]] + to_others(back_parts)
    out_rows = model_rows(hidden_parts, down_weight, 0)
    out_rows, back_parts[1:3] = lax.optimization_barrier((out_rows, back_parts[1:3]))
    back_own = added(back_parts)
    back_fwd = to_experts(out_rows)
    grad_own = (back_own * slope_own).astype(jnp.bfloat16)
    grad_rows = model_rows([grad_own] + from_others(grad_own), up_weight, 1)
    back_bwd = to_experts(grad_rows)

    both = matmul(pick_fwd, back_fwd)
    half = both.shape[0] // 2
    fwd_out = to_tokens(both[:half] + both[half:])
    fwd_out, back_bwd = lax.optimization_barrier((fwd_out, back_bwd))
    bwd_out = to_tokens(matmul(table_bwd, back_bwd))
    return (fwd_out[None], bwd_out[None])


def solution(mesh):
    sections, experts, parts = mesh.devices.shape
    split = (sections, experts // CORES, CORES, parts)
    mesh = Mesh(mesh.devices.reshape(split), ("section", "chip", "core", "dp"))
    expert = ("chip", "core")
    tokens = P("section", expert, "dp")
    routes = P("section", expert, None)
    return jax.shard_map(
        shards,
        mesh=mesh,
        in_specs=(
            tokens,
            routes,
            routes,
            tokens,
            routes,
            routes,
            P(expert, "dp", None),
            P(expert, None, "dp"),
            P("section", expert, None, None),
        ),
        out_specs=(tokens, tokens),
        check_vma=False,
    )
```

```python
import jax
import jax.numpy as jnp
from jax import lax
from jax.experimental import pallas as pl
from jax.experimental.pallas import tpu as pltpu
from jax.sharding import Mesh, PartitionSpec as P

CORES = 2
LANES = 128
VMEM_LIMIT = 48 * 1024 * 1024


def passed_along(block, axis, distance):
    devices = range(lax.axis_size(axis))
    route = [((i - distance) % len(devices), i) for i in devices]
    return lax.ppermute(block, axis, route)


def slot_targets(route_rows, experts, capacity):
    flat_routes = route_rows.reshape(-1)
    matches = (flat_routes[:, None] == jnp.arange(experts, dtype=jnp.int32)[None, :]).astype(
        jnp.int32
    )
    before = jnp.cumsum(matches, axis=0) - matches
    slot_rank = jnp.sum(before * matches, axis=1)
    return (flat_routes * capacity + slot_rank).reshape(route_rows.shape)


def chip_tables(targets, probs, rows, capacity):
    tokens, top_count = targets.shape
    core = lax.axis_index("core")
    other = jnp.arange(tokens, dtype=jnp.int32) // (tokens // CORES)
    group_core = jnp.where(other == 0, core, 1 - core)
    expert, place = targets // capacity, targets % capacity
    here = expert % CORES == core
    row = ((expert // CORES) * CORES + group_core[:, None]) * capacity + place
    row = jnp.where(here, row, -1)
    slots = jnp.arange(rows, dtype=jnp.int32)[None, :]
    filled = jnp.zeros((tokens, rows), jnp.bool_)
    shares = jnp.zeros((tokens, rows), jnp.float32)
    for k in range(top_count):
        match = row[:, k : k + 1] == slots
        filled = filled | match
        shares = jnp.where(match, probs[:, k : k + 1], shares)
    return filled.astype(jnp.bfloat16), shares


def silu_slope(pre_act):
    squash = jax.nn.sigmoid(pre_act)
    return squash * (1.0 + pre_act * (1.0 - squash))


def contract_last(left_rows, right_matrix):
    return lax.dot_general(
        left_rows, right_matrix, (((1,), (1,)), ((), ())), preferred_element_type=jnp.float32
    )


def matmul(left_rows, right_matrix):
    return jnp.dot(left_rows, right_matrix, preferred_element_type=jnp.float32)


def turned_own(array):
    size = array.shape[1] // lax.axis_size("dp")
    return lax.dynamic_slice_in_dim(array, lax.axis_index("dp") * size, size, axis=1)


def streamed(weight, dim, order, body, out_shape, inputs):
    parts = lax.axis_size("dp")
    size = weight.shape[dim] // parts
    shape = (size, weight.shape[1]) if dim == 0 else (weight.shape[0], size)

    def kernel(own, *refs):
        in_refs, weight_ref = refs[: len(inputs)], refs[len(inputs)]
        out_refs, blocks, arrived = refs[len(inputs) + 1 : -2], refs[-2], refs[-1]
        copies = []
        for j in range(parts):
            start = pl.multiple_of(order(own[0], j) * size, size)
            block = (
                weight_ref.at[pl.ds(start, size), :]
                if dim == 0
                else weight_ref.at[:, pl.ds(start, size)]
            )
            copies.append(pltpu.make_async_copy(block, blocks.at[j], arrived.at[j]))
            copies[j].start()
        carried = None
        for j in range(parts):
            copies[j].wait()
            carried = body(j, own[0], in_refs, blocks[j], out_refs, carried)

    return pl.pallas_call(
        kernel,
        out_shape=out_shape,
        in_specs=[pl.BlockSpec(memory_space=pltpu.SMEM)]
        + [pl.BlockSpec(memory_space=pltpu.VMEM)] * len(inputs)
        + [pl.BlockSpec(memory_space=pltpu.HBM)],
        out_specs=jax.tree.map(lambda _: pl.BlockSpec(memory_space=pltpu.VMEM), out_shape),
        scratch_shapes=[
            pltpu.VMEM((parts,) + shape, weight.dtype),
            pltpu.SemaphoreType.DMA((parts,)),
        ],
        compiler_params=pltpu.CompilerParams(vmem_limit_bytes=VMEM_LIMIT),
    )(lax.axis_index("dp").reshape(1), *inputs, pltpu.with_memory_space_constraint(weight, pltpu.HBM))


def turned(own, j):
    return lax.rem(own + j, lax.axis_size("dp"))


def product(left, right, dim):
    return lax.dot_general(
        left, right, (((1,), (dim,)), ((), ())), preferred_element_type=jnp.float32
    )


def hidden_blocks(rows, weight, dim):
    parts = lax.axis_size("dp")
    block = (rows.shape[0], weight.shape[dim] // parts)

    def body(j, own, in_refs, weight_block, out_refs, carried):
        out_refs[j][...] = product(in_refs[0][...], weight_block, 1 - dim).astype(
            out_refs[j].dtype
        )

    kinds = [jnp.float32] + [jnp.bfloat16] * (parts - 1)
    out_shape = [jax.ShapeDtypeStruct(block, kind) for kind in kinds]
    return list(streamed(weight, dim, turned, body, out_shape, [rows]))


def ranked_blocks(rows, weight):
    parts = lax.axis_size("dp")
    block = (rows.shape[0], weight.shape[0] // parts)

    def body(j, own, in_refs, weight_block, out_refs, carried):
        result = product(in_refs[0][...], weight_block, 1)
        out_refs[1][j] = result.astype(jnp.bfloat16)

        @pl.when(own == j)
        def _():
            out_refs[0][...] = result

    out_shape = [
        jax.ShapeDtypeStruct(block, jnp.float32),
        jax.ShapeDtypeStruct((parts,) + block, jnp.bfloat16),
    ]
    return streamed(weight, 0, lambda own, j: j, body, out_shape, [rows])


def model_rows(hidden_parts, weight, dim):
    parts = len(hidden_parts)
    out_shape = (hidden_parts[0].shape[0], weight.shape[1 - dim])

    def body(j, own, in_refs, weight_block, out_refs, carried):
        result = product(in_refs[j][...], weight_block, dim)
        total = result if carried is None else carried + result
        if j == parts - 1:
            out_refs[0][...] = total.astype(jnp.bfloat16)
        return total

    out_shape = jax.ShapeDtypeStruct(out_shape, jnp.bfloat16)
    return streamed(weight, dim, turned, body, out_shape, hidden_parts)


def summed_at_once(total, blocks):
    own = lax.axis_index("dp")
    blocks = lax.all_to_all(blocks, "dp", split_axis=0, concat_axis=0, tiled=True)
    for rank in range(blocks.shape[0]):
        total = total + jnp.where(own == rank, 0.0, blocks[rank].astype(jnp.float32))
    return total


def to_others(partials):
    return [
        passed_along(partials[j].astype(jnp.bfloat16), "dp", j) for j in range(1, len(partials))
    ]


def from_others(block):
    return [passed_along(block, "dp", -j) for j in range(1, lax.axis_size("dp"))]


def added(parts):
    total = parts[0]
    for part in parts[1:]:
        total = total + part.astype(jnp.float32)
    return total


def halves(values):
    coarse = lax.reduce_precision(values, 8, 7)
    return coarse.astype(jnp.bfloat16), (values - coarse).astype(jnp.bfloat16)


def contract_first(left_rows, right_rows):
    return lax.dot_general(
        left_rows, right_rows, (((0,), (0,)), ((), ())), preferred_element_type=jnp.float32
    )


def labels(targets, probs, pieces):
    fields = [targets.astype(jnp.bfloat16)]
    for _ in range(pieces):
        piece = lax.reduce_precision(probs, 8, 7)
        fields.append(piece.astype(jnp.bfloat16))
        probs = probs - piece
    fields = jnp.concatenate(fields, axis=1)
    return jnp.pad(fields, ((0, 0), (0, LANES - fields.shape[1])))


def with_other_core(rows, label, top_count, pieces):
    message = jnp.concatenate([rows, label], axis=1)
    other = passed_along(message, "core", 1)
    width = rows.shape[1]
    both = jnp.concatenate([rows, other[:, :width]], axis=0)
    label = jnp.concatenate([label, other[:, width:]], axis=0).astype(jnp.float32)
    targets = label[:, :top_count].astype(jnp.int32)
    probs = label[:, top_count : 2 * top_count]
    for k in range(2, pieces + 1):
        probs = probs + label[:, k * top_count : (k + 1) * top_count]
    return both, targets, probs


def shards(
    fwd_act, fwd_routes, fwd_probs, bwd_grad, bwd_routes, bwd_probs, w_up, w_down, act_stash
):
    chips = lax.axis_size("chip")
    experts = chips * lax.axis_size("core")
    tokens_here, width_part = fwd_act.shape[1:]
    rows = act_stash.shape[2]
    capacity = rows // experts

    def to_experts(block):
        block = block.reshape(chips, rows // chips, width_part)
        block = lax.all_to_all(block, "chip", split_axis=0, concat_axis=0, tiled=True)
        return block.reshape(rows, width_part)

    def to_tokens(part):
        other = passed_along(part[tokens_here:], "core", 1)
        return (part[:tokens_here] + other).astype(jnp.bfloat16)

    arriving = passed_along(fwd_act[0], "section", 1)
    top_count = fwd_routes.shape[2]
    label_fwd = labels(slot_targets(fwd_routes[0], experts, capacity), fwd_probs[0], 2)
    tokens_fwd, targets_fwd, probs_fwd = with_other_core(arriving, label_fwd, top_count, 2)
    table_fwd, shares_fwd = chip_tables(targets_fwd, probs_fwd, rows, capacity)
    pick_fwd = jnp.concatenate(halves(shares_fwd), axis=0)

    sent_fwd = contract_first(table_fwd, tokens_fwd).astype(jnp.bfloat16)
    sent_fwd, grad_in = lax.optimization_barrier((sent_fwd, bwd_grad[0]))
    recv_fwd = to_experts(sent_fwd)

    label_bwd = labels(slot_targets(bwd_routes[0], experts, capacity), bwd_probs[0], 3)
    incoming = passed_along(grad_in, "section", -1)
    incoming, targets_bwd, probs_bwd = with_other_core(incoming, label_bwd, top_count, 3)
    table_bwd, shares_bwd = chip_tables(targets_bwd, probs_bwd, rows, capacity)
    slot_probs = jnp.sum(shares_bwd, axis=0)[:, None]
    sent_bwd = (slot_probs * contract_first(table_bwd, incoming)).astype(jnp.bfloat16)
    stash_own = turned_own(act_stash[0, 0])
    slope_own = silu_slope(stash_own.astype(jnp.float32))
    sent_bwd, slope_own = lax.optimization_barrier((sent_bwd, slope_own))
    recv_bwd = to_experts(sent_bwd)

    up_weight, down_weight = w_up[0], w_down[0]
    pre_parts = hidden_blocks(recv_fwd, up_weight, 1)
    pre_own = added([pre_parts[0]] + to_others(pre_parts))
    hidden_own = jax.nn.silu(pre_own).astype(jnp.bfloat16)
    hidden_parts = [hidden_own] + from_others(hidden_own)
    hidden_parts[2], recv_bwd = lax.optimization_barrier((hidden_parts[2], recv_bwd))
    back_parts = hidden_blocks(recv_bwd, down_weight, 0)
    back_parts = [back_parts[0]] + to_others(back_parts)
    out_rows = model_rows(hidden_parts, down_weight, 0)
    out_rows, back_parts = lax.optimization_barrier((out_rows, back_parts))
    back_own = added(back_parts)
    back_fwd = to_experts(out_rows)
    grad_own = (back_own * slope_own).astype(jnp.bfloat16)
    grad_rows = model_rows([grad_own] + from_others(grad_own), up_weight, 1)
    back_bwd = to_experts(grad_rows)

    both = matmul(pick_fwd, back_fwd)
    half = both.shape[0] // 2
    fwd_out = to_tokens(both[:half] + both[half:])
    fwd_out, back_bwd = lax.optimization_barrier((fwd_out, back_bwd))
    bwd_out = to_tokens(matmul(table_bwd, back_bwd))
    return (fwd_out[None], bwd_out[None])


def solution(mesh):
    sections, experts, parts = mesh.devices.shape
    split = (sections, experts // CORES, CORES, parts)
    mesh = Mesh(mesh.devices.reshape(split), ("section", "chip", "core", "dp"))
    expert = ("chip", "core")
    tokens = P("section", expert, "dp")
    routes = P("section", expert, None)
    return jax.shard_map(
        shards,
        mesh=mesh,
        in_specs=(
            tokens,
            routes,
            routes,
            tokens,
            routes,
            routes,
            P(expert, "dp", None),
            P(expert, None, "dp"),
            P("section", expert, None, None),
        ),
        out_specs=(tokens, tokens),
        check_vma=False,
    )
```

```python
import jax
import jax.numpy as jnp
from jax import lax
from jax.experimental import pallas as pl
from jax.experimental.pallas import tpu as pltpu
from jax.sharding import Mesh, PartitionSpec as P

CORES = 2
LANES = 128
VMEM_LIMIT = 48 * 1024 * 1024


def passed_along(block, axis, distance):
    devices = range(lax.axis_size(axis))
    route = [((i - distance) % len(devices), i) for i in devices]
    return lax.ppermute(block, axis, route)


def slot_targets(route_rows, experts, capacity):
    flat_routes = route_rows.reshape(-1)
    matches = (flat_routes[:, None] == jnp.arange(experts, dtype=jnp.int32)[None, :]).astype(
        jnp.int32
    )
    before = jnp.cumsum(matches, axis=0) - matches
    slot_rank = jnp.sum(before * matches, axis=1)
    return (flat_routes * capacity + slot_rank).reshape(route_rows.shape)


def chip_tables(targets, probs, rows, capacity):
    tokens, top_count = targets.shape
    core = lax.axis_index("core")
    other = jnp.arange(tokens, dtype=jnp.int32) // (tokens // CORES)
    group_core = jnp.where(other == 0, core, 1 - core)
    expert, place = targets // capacity, targets % capacity
    here = expert % CORES == core
    row = ((expert // CORES) * CORES + group_core[:, None]) * capacity + place
    row = jnp.where(here, row, -1)
    slots = jnp.arange(rows, dtype=jnp.int32)[None, :]
    filled = jnp.zeros((tokens, rows), jnp.bool_)
    shares = jnp.zeros((tokens, rows), jnp.float32)
    for k in range(top_count):
        match = row[:, k : k + 1] == slots
        filled = filled | match
        shares = jnp.where(match, probs[:, k : k + 1], shares)
    return filled.astype(jnp.bfloat16), shares


def silu_slope(pre_act):
    squash = jax.nn.sigmoid(pre_act)
    return squash * (1.0 + pre_act * (1.0 - squash))


def contract_last(left_rows, right_matrix):
    return lax.dot_general(
        left_rows, right_matrix, (((1,), (1,)), ((), ())), preferred_element_type=jnp.float32
    )


def matmul(left_rows, right_matrix):
    return jnp.dot(left_rows, right_matrix, preferred_element_type=jnp.float32)


def turned_own(array):
    size = array.shape[1] // lax.axis_size("dp")
    return lax.dynamic_slice_in_dim(array, lax.axis_index("dp") * size, size, axis=1)


def streamed(weight, dim, order, body, out_shape, inputs):
    parts = lax.axis_size("dp")
    size = weight.shape[dim] // parts
    shape = (size, weight.shape[1]) if dim == 0 else (weight.shape[0], size)

    def kernel(own, *refs):
        in_refs, weight_ref = refs[: len(inputs)], refs[len(inputs)]
        out_refs, blocks, arrived = refs[len(inputs) + 1 : -2], refs[-2], refs[-1]
        copies = []
        for j in range(parts):
            start = pl.multiple_of(order(own[0], j) * size, size)
            block = (
                weight_ref.at[pl.ds(start, size), :]
                if dim == 0
                else weight_ref.at[:, pl.ds(start, size)]
            )
            copies.append(pltpu.make_async_copy(block, blocks.at[j], arrived.at[j]))
            copies[j].start()
        carried = None
        for j in range(parts):
            copies[j].wait()
            carried = body(j, own[0], in_refs, blocks[j], out_refs, carried)

    return pl.pallas_call(
        kernel,
        out_shape=out_shape,
        in_specs=[pl.BlockSpec(memory_space=pltpu.SMEM)]
        + [pl.BlockSpec(memory_space=pltpu.VMEM)] * len(inputs)
        + [pl.BlockSpec(memory_space=pltpu.HBM)],
        out_specs=jax.tree.map(lambda _: pl.BlockSpec(memory_space=pltpu.VMEM), out_shape),
        scratch_shapes=[
            pltpu.VMEM((parts,) + shape, weight.dtype),
            pltpu.SemaphoreType.DMA((parts,)),
        ],
        compiler_params=pltpu.CompilerParams(vmem_limit_bytes=VMEM_LIMIT),
    )(lax.axis_index("dp").reshape(1), *inputs, pltpu.with_memory_space_constraint(weight, pltpu.HBM))


def turned(own, j):
    return lax.rem(own + j, lax.axis_size("dp"))


def product(left, right, dim):
    return lax.dot_general(
        left, right, (((1,), (dim,)), ((), ())), preferred_element_type=jnp.float32
    )


def hidden_blocks(rows, weight, dim):
    parts = lax.axis_size("dp")
    block = (rows.shape[0], weight.shape[dim] // parts)

    def body(j, own, in_refs, weight_block, out_refs, carried):
        out_refs[j][...] = product(in_refs[0][...], weight_block, 1 - dim).astype(
            out_refs[j].dtype
        )

    kinds = [jnp.float32] + [jnp.bfloat16] * (parts - 1)
    out_shape = [jax.ShapeDtypeStruct(block, kind) for kind in kinds]
    return list(streamed(weight, dim, turned, body, out_shape, [rows]))


def ranked_blocks(rows, weight):
    parts = lax.axis_size("dp")
    block = (rows.shape[0], weight.shape[0] // parts)

    def body(j, own, in_refs, weight_block, out_refs, carried):
        result = product(in_refs[0][...], weight_block, 1)
        out_refs[1][j] = result.astype(jnp.bfloat16)

        @pl.when(own == j)
        def _():
            out_refs[0][...] = result

    out_shape = [
        jax.ShapeDtypeStruct(block, jnp.float32),
        jax.ShapeDtypeStruct((parts,) + block, jnp.bfloat16),
    ]
    return streamed(weight, 0, lambda own, j: j, body, out_shape, [rows])


def model_rows(hidden_parts, weight, dim):
    parts = len(hidden_parts)
    out_shape = (hidden_parts[0].shape[0], weight.shape[1 - dim])

    def body(j, own, in_refs, weight_block, out_refs, carried):
        result = product(in_refs[j][...], weight_block, dim)
        total = result if carried is None else carried + result
        if j == parts - 1:
            out_refs[0][...] = total.astype(jnp.bfloat16)
        return total

    out_shape = jax.ShapeDtypeStruct(out_shape, jnp.bfloat16)
    return streamed(weight, dim, turned, body, out_shape, hidden_parts)


def summed_at_once(total, blocks):
    own = lax.axis_index("dp")
    blocks = lax.all_to_all(blocks, "dp", split_axis=0, concat_axis=0, tiled=True)
    for rank in range(blocks.shape[0]):
        total = total + jnp.where(own == rank, 0.0, blocks[rank].astype(jnp.float32))
    return total


def to_others(partials):
    return [
        passed_along(partials[j].astype(jnp.bfloat16), "dp", j) for j in range(1, len(partials))
    ]


def from_others(block):
    return [passed_along(block, "dp", -j) for j in range(1, lax.axis_size("dp"))]


def added(parts):
    total = parts[0]
    for part in parts[1:]:
        total = total + part.astype(jnp.float32)
    return total


def halves(values):
    coarse = lax.reduce_precision(values, 8, 7)
    return coarse.astype(jnp.bfloat16), (values - coarse).astype(jnp.bfloat16)


def contract_first(left_rows, right_rows):
    return lax.dot_general(
        left_rows, right_rows, (((0,), (0,)), ((), ())), preferred_element_type=jnp.float32
    )


def labels(targets, probs, pieces):
    fields = [targets.astype(jnp.bfloat16)]
    for _ in range(pieces):
        piece = lax.reduce_precision(probs, 8, 7)
        fields.append(piece.astype(jnp.bfloat16))
        probs = probs - piece
    fields = jnp.concatenate(fields, axis=1)
    return jnp.pad(fields, ((0, 0), (0, LANES - fields.shape[1])))


def with_other_core(rows, label, top_count, pieces):
    message = jnp.concatenate([rows, label], axis=1)
    other = passed_along(message, "core", 1)
    width = rows.shape[1]
    both = jnp.concatenate([rows, other[:, :width]], axis=0)
    label = jnp.concatenate([label, other[:, width:]], axis=0).astype(jnp.float32)
    targets = label[:, :top_count].astype(jnp.int32)
    probs = label[:, top_count : 2 * top_count]
    for k in range(2, pieces + 1):
        probs = probs + label[:, k * top_count : (k + 1) * top_count]
    return both, targets, probs


def shards(
    fwd_act, fwd_routes, fwd_probs, bwd_grad, bwd_routes, bwd_probs, w_up, w_down, act_stash
):
    chips = lax.axis_size("chip")
    experts = chips * lax.axis_size("core")
    tokens_here, width_part = fwd_act.shape[1:]
    rows = act_stash.shape[2]
    capacity = rows // experts

    def to_experts(block):
        block = block.reshape(chips, rows // chips, width_part)
        block = lax.all_to_all(block, "chip", split_axis=0, concat_axis=0, tiled=True)
        return block.reshape(rows, width_part)

    def to_tokens(part):
        other = passed_along(part[tokens_here:].astype(jnp.bfloat16), "core", 1)
        return (part[:tokens_here] + other.astype(jnp.float32)).astype(jnp.bfloat16)

    arriving = passed_along(fwd_act[0], "section", 1)
    top_count = fwd_routes.shape[2]
    label_fwd = labels(slot_targets(fwd_routes[0], experts, capacity), fwd_probs[0], 2)
    tokens_fwd, targets_fwd, probs_fwd = with_other_core(arriving, label_fwd, top_count, 2)
    table_fwd, shares_fwd = chip_tables(targets_fwd, probs_fwd, rows, capacity)
    pick_fwd = jnp.concatenate(halves(shares_fwd), axis=0)

    sent_fwd = contract_first(table_fwd, tokens_fwd).astype(jnp.bfloat16)
    sent_fwd, grad_in = lax.optimization_barrier((sent_fwd, bwd_grad[0]))
    recv_fwd = to_experts(sent_fwd)

    label_bwd = labels(slot_targets(bwd_routes[0], experts, capacity), bwd_probs[0], 3)
    incoming = passed_along(grad_in, "section", -1)
    incoming, targets_bwd, probs_bwd = with_other_core(incoming, label_bwd, top_count, 3)
    table_bwd, shares_bwd = chip_tables(targets_bwd, probs_bwd, rows, capacity)
    slot_probs = jnp.sum(shares_bwd, axis=0)[:, None]
    sent_bwd = (slot_probs * contract_first(table_bwd, incoming)).astype(jnp.bfloat16)
    stash_own = turned_own(act_stash[0, 0])
    slope_own = silu_slope(stash_own.astype(jnp.float32))
    sent_bwd, slope_own = lax.optimization_barrier((sent_bwd, slope_own))
    recv_bwd = to_experts(sent_bwd)

    up_weight, down_weight = w_up[0], w_down[0]
    pre_parts = hidden_blocks(recv_fwd, up_weight, 1)
    pre_own = added([pre_parts[0]] + to_others(pre_parts))
    hidden_own = jax.nn.silu(pre_own).astype(jnp.bfloat16)
    hidden_parts = [hidden_own] + from_others(hidden_own)
    hidden_parts[2], recv_bwd = lax.optimization_barrier((hidden_parts[2], recv_bwd))
    back_parts = hidden_blocks(recv_bwd, down_weight, 0)
    back_parts = [back_parts[0]] + to_others(back_parts)
    out_rows = model_rows(hidden_parts, down_weight, 0)
    out_rows, back_parts = lax.optimization_barrier((out_rows, back_parts))
    back_own = added(back_parts)
    back_fwd = to_experts(out_rows)
    grad_own = (back_own * slope_own).astype(jnp.bfloat16)
    grad_rows = model_rows([grad_own] + from_others(grad_own), up_weight, 1)
    back_bwd = to_experts(grad_rows)

    both = matmul(pick_fwd, back_fwd)
    half = both.shape[0] // 2
    fwd_out = to_tokens(both[:half] + both[half:])
    fwd_out, back_bwd = lax.optimization_barrier((fwd_out, back_bwd))
    bwd_out = to_tokens(matmul(table_bwd, back_bwd))
    return (fwd_out[None], bwd_out[None])


def solution(mesh):
    sections, experts, parts = mesh.devices.shape
    split = (sections, experts // CORES, CORES, parts)
    mesh = Mesh(mesh.devices.reshape(split), ("section", "chip", "core", "dp"))
    expert = ("chip", "core")
    tokens = P("section", expert, "dp")
    routes = P("section", expert, None)
    return jax.shard_map(
        shards,
        mesh=mesh,
        in_specs=(
            tokens,
            routes,
            routes,
            tokens,
            routes,
            routes,
            P(expert, "dp", None),
            P(expert, None, "dp"),
            P("section", expert, None, None),
        ),
        out_specs=(tokens, tokens),
        check_vma=False,
    )
```
